256 devices in a mesh: seq: 32 (over y, z), head: 8 (over x, core).
Axes of the slice: x: 4, y: 4, z: 8, core: 2. Of those that a mesh axis runs over, the one named last changes fastest.
Arguments:
- tokens: bfloat16 [8192, 2048], P('seq'), may hold values from -12 to 12
- w_qk: bfloat16 [2048, 2, 2048], P(None, None, 'head'), may hold values from -0.125 to 0.125
- w_vz: bfloat16 [2048, 2, 4096], P(None, None, 'head'), may hold values from -0.125 to 0.125
- w_ab: bfloat16 [2048, 2, 32], P(None, None, 'head'), may hold values from -1 to 1
- conv_qk: float32 [4, 2, 2048], P(None, None, 'head'), may hold values from -3 to 3
- conv_v: float32 [4, 4096], P(None, 'head'), may hold values from -3 to 3
- a_log: float32 [32], P('head'), may hold values from -4 to -1
- dt_bias: float32 [32], P('head'), may hold values from -13 to 2
- beta_bias: float32 [32], P('head'), may hold values from -7 to 1
- norm_gain: float32 [128], replicated, may hold values from 0.1 to 1.9
- w_out: bfloat16 [4096, 2048], P('head'), may hold values from -0.125 to 0.125
Outputs:
- mixed: bfloat16 [8192, 2048], P('seq', 'head')
The draws below stay inside these ranges and needn't reach their ends.
All inputs are finite; a program needn't handle non-finite values.
Results may differ from the reference program's by a relative error of at most 0.0049.
Values sent between devices are 32-bit elements; how exact they have to be, the bound alone decides.
No kernel may reach another device: no remote copies, remote signals or barrier semaphores. Data moves between devices by JAX's collectives and lax.ppermute only.
A program may use at most 128 MiB of HBM per device.

```python
import math
import jax
import jax.numpy as jnp
from jax import lax

D = 2048
MATCHING_COUNT = 16
V_HEADS = 32
DK = 128
DV = 128
KW = 4
TOKENS = 8192


def block_direction_column(key):
    signs = jax.random.bernoulli(jax.random.fold_in(key, 202), 0.5, (D,))
    return jnp.where(signs, 1.0, -1.0).astype(jnp.float32)


def head_laws(key, share):
    slow = jax.random.uniform(jax.random.fold_in(key, 11), (V_HEADS,)) < share
    fast_rate = jax.random.uniform(jax.random.fold_in(key, 12), (V_HEADS,), minval=0.02, maxval=0.06)
    slow_rate = jax.random.uniform(jax.random.fold_in(key, 13), (V_HEADS,), minval=0.1, maxval=0.3)
    rate = jnp.where(slow, slow_rate, fast_rate)
    kept = jax.random.uniform(jax.random.fold_in(key, 14), (V_HEADS,), minval=0.2, maxval=0.8)
    erased = jax.random.uniform(jax.random.fold_in(key, 15), (V_HEADS,), minval=0.5, maxval=1.5)
    fast_beta = jax.random.uniform(jax.random.fold_in(key, 16), (V_HEADS,), minval=-1.0, maxval=1.0)
    fast_bias = jax.random.uniform(jax.random.fold_in(key, 17), (V_HEADS,), minval=0.0, maxval=1.0)
    return (slow, rate, kept, erased, fast_beta, fast_bias)


def draw_tokens(key, part):
    direction_column = block_direction_column(key)
    key = jax.random.fold_in(key, 3)
    base = jax.random.normal(key, (TOKENS, D))
    places = jax.random.randint(jax.random.fold_in(key, 4), (6,), 0, TOKENS)
    struck = jnp.any(jnp.arange(TOKENS)[:, None] == places[None, :], 1)
    lift = 33.3 / math.sqrt(D)
    return (base + jnp.where(struck[:, None], lift * direction_column[None, :], 0.0)).astype(jnp.bfloat16)


def draw_w_ab(key, part):
    direction_column = block_direction_column(key)
    key = jax.random.fold_in(key, 5)
    spread = jax.random.normal(key, (D, 2, V_HEADS)) / math.sqrt(D)
    scales = jnp.array([0.5, 0.3], jnp.float32).reshape(1, 2, 1)
    shared = jnp.stack([jnp.zeros((D,), jnp.float32), direction_column], 1)[:, :, None] * (0.3 / math.sqrt(D))
    return (spread * scales + shared).astype(jnp.bfloat16)


def draw_a_log(key, part):
    share = 0.5
    slow, rate, kept, erased, fast_beta, fast_bias = head_laws(key, share)
    return jnp.log(rate)


def draw_dt_bias(key, part):
    share = 0.5
    slow, rate, kept, erased, fast_beta, fast_bias = head_laws(key, share)
    slow_bias = jnp.log(jnp.expm1(kept / (rate * TOKENS)))
    return jnp.where(slow, slow_bias, fast_bias)


def draw_beta_bias(key, part):
    share = 0.5
    slow, rate, kept, erased, fast_beta, fast_bias = head_laws(key, share)
    strength = erased * DK / TOKENS
    return jnp.where(slow, jnp.log(strength / (1.0 - strength)), fast_beta)


def strengthened(values, own_key, source, target, shards_of, factor):
    owner, partner = [(jnp.arange(values.shape[dim]) // (values.shape[dim] // shards_of)).reshape([-1 if axis == dim else 1 for axis in range(values.ndim)]) for dim in (source, target)]
    chosen = jax.random.permutation(own_key, shards_of)[partner]
    strong = (owner == chosen) | (owner == (partner + shards_of // 2) % shards_of)
    return jnp.where(strong, factor * values, values)


def shard_levels(rng, dims, shards, smallest, top_value):
    gain, own = 1.0, jax.random.fold_in(rng, 6)
    for dim, parts in shards:
        heights = jnp.exp(jax.random.uniform(jax.random.fold_in(own, dim), (parts,), jnp.float32, smallest / len(shards), top_value / len(shards)))
        gain = gain * jnp.repeat(heights, dims[dim] // parts).reshape([-1 if axis == dim else 1 for axis in range(len(dims))])
    return gain


def bell_draw(key, dims, width, reach, cuts=(), held_as=jnp.bfloat16):
    result = jax.random.normal(key, dims, jnp.float32) * width
    if len(cuts) > 0:
        result = shard_levels(key, dims, cuts, -0.22, 0.18) * result
    return jnp.clip(result, min=-reach, max=reach).astype(held_as)


def noise_with(own_key, extent, deviation, bound, split, heavy, dtype=jnp.bfloat16):
    entries = deviation * jax.random.normal(own_key, extent, jnp.float32)
    if split:
        entries = entries * shard_levels(own_key, extent, split, -0.22, 0.18)
    return jnp.clip(strengthened(entries, jax.random.fold_in(own_key, 3), *heavy), -bound, bound).astype(dtype)


def setup_inputs(seed: int = 0) -> dict:
    streams_of = jax.random.split(jax.random.key(seed), 12)
    tokens = draw_tokens(jax.random.fold_in(streams_of[11], 71), 0)
    w_qk = bell_draw(streams_of[1], (D, 2, MATCHING_COUNT * DK), D ** -0.5, 0.125, ((2, 8),))
    w_vz = bell_draw(streams_of[2], (D, 2, V_HEADS * DV), D ** -0.5, 0.125, ((2, 8),))
    w_ab = draw_w_ab(jax.random.fold_in(streams_of[11], 71), 0)
    conv_qk = bell_draw(streams_of[4], (KW, 2, MATCHING_COUNT * DK), 0.5, 3.0, ((2, 8),), jnp.float32)
    conv_v = bell_draw(streams_of[5], (KW, V_HEADS * DV), 0.5, 3.0, ((1, 8),), jnp.float32)
    a_log = draw_a_log(jax.random.fold_in(streams_of[11], 71), 0)
    dt_bias = draw_dt_bias(jax.random.fold_in(streams_of[11], 71), 0)
    beta_bias = draw_beta_bias(jax.random.fold_in(streams_of[11], 71), 0)
    norm_gain = jnp.clip(1.0 + 0.18 * jax.random.normal(streams_of[9], (DV,), jnp.float32), 0.1, 1.9)
    w_out = noise_with(streams_of[10], (V_HEADS * DV, D), (V_HEADS * DV) ** -0.5, 0.125, ((0, 8),), (0, 1, 8, 2.0))
    return {"tokens": tokens, "w_qk": w_qk, "w_vz": w_vz, "w_ab": w_ab, "conv_qk": conv_qk, "conv_v": conv_v, "a_log": a_log, "dt_bias": dt_bias, "beta_bias": beta_bias, "norm_gain": norm_gain, "w_out": w_out}


highest_setting = lax.Precision.HIGHEST

def unit_rows(vectors):
    return vectors * lax.rsqrt(lax.optimization_barrier(jnp.sum(vectors * vectors, -1, keepdims=True)) + 1e-06)

def causal_conv(channels, taps):
    kernel_len = taps.shape[0]
    tok_count = channels.shape[0]
    padded = jnp.concatenate([jnp.zeros((kernel_len - 1, channels.shape[1]), jnp.float32), channels], 0)
    conv_sum = padded[0:tok_count] * taps[0]
    for offset in range(1, kernel_len):
        conv_sum = conv_sum + padded[offset:offset + tok_count] * taps[offset]
    return jax.nn.silu(conv_sum)

def advance(current_state, inputs_now):
    current_query, current_key, value_now, beta_now, decay_now = inputs_now
    current_state = jnp.exp(decay_now)[:, None, None] * current_state
    recalled_values = jnp.einsum('wi,wis->ws', current_key, current_state, precision=highest_setting)
    current_state = current_state + (beta_now[:, None] * current_key)[:, :, None] * (value_now - recalled_values)[:, None, :]
    return (current_state, jnp.einsum('wi,wis->ws', current_query, current_state, precision=highest_setting))

def reference(tokens, w_qk, w_vz, w_ab, conv_qk, conv_v, a_log, dt_bias, beta_bias, norm_gain, w_out):
    tok_count = tokens.shape[0]
    inputs = tokens.astype(jnp.float32)
    proj_qk = jnp.einsum('td,dcf->tcf', inputs, w_qk.astype(jnp.float32), precision=highest_setting)
    proj_vz = jnp.einsum('td,dcf->tcf', inputs, w_vz.astype(jnp.float32), precision=highest_setting)
    proj_ab = jnp.einsum('td,dcf->tcf', inputs, w_ab.astype(jnp.float32), precision=highest_setting)
    qk_width = MATCHING_COUNT * DK
    channels = jnp.concatenate([proj_qk.reshape(tok_count, 2 * qk_width), proj_vz[:, 0]], 1)
    taps = jnp.concatenate([conv_qk.reshape(KW, 2 * qk_width), conv_v], 1)
    conv_out = causal_conv(channels, taps)
    group_size = V_HEADS // MATCHING_COUNT
    query_rows = jnp.repeat(unit_rows(conv_out[:, :qk_width].reshape(tok_count, MATCHING_COUNT, DK)), group_size, axis=1) * DK ** (-0.5)
    key_rows = jnp.repeat(unit_rows(conv_out[:, qk_width:2 * qk_width].reshape(tok_count, MATCHING_COUNT, DK)), group_size, axis=1)
    value_rows = conv_out[:, 2 * qk_width:].reshape(tok_count, V_HEADS, DV)
    beta_rows = jax.nn.sigmoid(proj_ab[:, 0] + beta_bias)
    log_decay = -jnp.exp(a_log) * jax.nn.softplus(proj_ab[:, 1] + dt_bias)
    start_state = jnp.zeros((V_HEADS, DK, DV), jnp.float32)
    final_state, core = lax.scan(advance, start_state, (query_rows, key_rows, value_rows, beta_rows, log_decay))
    gates = proj_vz[:, 1].reshape(tok_count, V_HEADS, DV)
    normed = core * lax.rsqrt(lax.optimization_barrier(jnp.mean(core * core, -1, keepdims=True)) + 1e-06) * norm_gain * jax.nn.silu(gates)
    normed = normed.astype(jnp.bfloat16).reshape(tok_count, V_HEADS * DV)
    return jnp.dot(normed, w_out, preferred_element_type=jnp.float32).astype(jnp.bfloat16)
```

```python
import functools

import jax
import jax.numpy as jnp
from jax import lax
from jax.experimental import pallas as pl
from jax.experimental.pallas import tpu as pltpu
from jax.sharding import Mesh, PartitionSpec as P

F32 = jnp.float32
BF16 = jnp.bfloat16
DK = 128
DV = 128
HALF = 128
SEG = 256
VH = 4
QKH = 2
EPS = 1e-06
FLOOR = -110.0

VMEM = pl.BlockSpec(memory_space=pltpu.VMEM)
SMEM = pl.BlockSpec(memory_space=pltpu.SMEM)


def params(mib):
    return pltpu.CompilerParams(vmem_limit_bytes=mib * 1024 * 1024)


def split2(x):
    hi = x.astype(BF16)
    return hi, (x - hi.astype(F32)).astype(BF16)


def split3(x):
    hi = x.astype(BF16)
    rest = x - hi.astype(F32)
    mid = rest.astype(BF16)
    return hi, mid, (rest - mid.astype(F32)).astype(BF16)


def mm(a, b):
    return jnp.dot(a, b, preferred_element_type=F32)


def mm_nt(a, b):
    return lax.dot_general(a, b, (((1,), (1,)), ((), ())), preferred_element_type=F32)


def dot3(a, b):
    ah, al = split2(a)
    bh, bl = split2(b)
    return mm(jnp.concatenate([ah, al, ah], 1), jnp.concatenate([bh, bh, bl], 0))


def dot3_nt(a, b):
    ah, al = split2(a)
    bh, bl = split2(b)
    return mm_nt(jnp.concatenate([ah, al, ah], 1), jnp.concatenate([bh, bh, bl], 1))


def spread_blocks(x):
    zero = jnp.zeros((HALF, HALF), x.dtype)
    return jnp.concatenate(
        [
            jnp.concatenate([x[:, :HALF], zero], 1),
            jnp.concatenate([zero, x[:, HALF:]], 1),
        ],
        0,
    )


def dot3_blocks(a, b):
    ah, al = split2(a)
    bh, bl = split2(b)
    bh, bl = spread_blocks(bh), spread_blocks(bl)
    return mm(jnp.concatenate([ah, al, ah], 1), jnp.concatenate([bh, bh, bl], 0))


def iota2(shape, dim):
    return lax.broadcasted_iota(jnp.int32, shape, dim)


def silu(x):
    return x / (1.0 + jnp.exp(-x))


def softplus(x):
    return jnp.maximum(x, 0.0) + jnp.log1p(jnp.exp(-jnp.abs(x)))


def unit(x):
    return x * lax.rsqrt(jnp.sum(x * x, -1, keepdims=True) + EPS)


def fades(decay_col, lower):
    rows, cols = iota2((SEG, SEG), 0), iota2((SEG, SEG), 1)
    terms = jnp.where(rows > cols, jnp.broadcast_to(decay_col, (SEG, SEG)), 0.0)
    hi, mid, lo = split3(terms)
    return jnp.exp(mm(lower, hi) + mm(lower, mid) + mm(lower, lo))


def lower_ones():
    rows, cols = iota2((SEG, SEG), 0), iota2((SEG, SEG), 1)
    return jnp.where(rows >= cols, 1.0, 0.0).astype(BF16)


def segment_kernel(
    place, a_log, dt_bias, beta_bias, qk, vz, halo, taps_qk, taps_v, ab,
    out0, out1, out2, out3, q_out, k_out, ef_out, cols_out,
    pad, maps,
):
    rows, cols = iota2((SEG, SEG), 0), iota2((SEG, SEG), 1)
    pad[0:8, :] = halo[...]
    pad[8:, 0:256] = qk[0]
    pad[8:, 256:512] = qk[1]
    pad[8:, 512:1024] = vz[0]

    def conv(start, width, tap):
        total = None
        for j in range(4):
            term = pad[5 + j : 5 + j + SEG, start : start + width] * tap(j)
            total = term if total is None else total + term
        return silu(total)

    head_rows = []
    for h in range(VH):
        head_rows.append(jax.nn.sigmoid(ab[0, h : h + 1, :] + beta_bias[h]))
    for h in range(VH):
        rate = jnp.exp(jnp.full((1, SEG), a_log[h], F32))
        head_rows.append(
            jnp.maximum(-rate * softplus(ab[1, h : h + 1, :] + dt_bias[h]), FLOOR)
        )
    col8 = jnp.concatenate(head_rows, 0).T
    cols_out[...] = col8
    lower = lower_ones()
    later = jnp.where(rows < cols, 1.0, 0.0).astype(BF16)
    dhi, dmid, dlo = split3(col8)
    growth8 = jnp.exp(mm(lower, dhi) + mm(lower, dmid) + mm(lower, dlo))
    closing8 = jnp.exp(mm(later, dhi) + mm(later, dmid) + mm(later, dlo))

    prow, pcol = iota2((HALF, SEG), 0), iota2((HALF, SEG), 1) & (HALF - 1)
    strict_pair = prow > pcol
    eye_pair = jnp.where(prow == pcol, 1.0, 0.0)
    eye = jnp.where(iota2((DK, DK), 0) == iota2((DK, DK), 1), 1.0, 0.0)

    for g in range(QKH):
        q = unit(conv(g * DK, DK, lambda j: taps_qk[j, 0:1, g * DK : (g + 1) * DK])) * DK ** -0.5
        k = unit(conv(256 + g * DK, DK, lambda j: taps_qk[j, 1:2, g * DK : (g + 1) * DK]))
        q_out[g] = q
        k_out[g] = k
        kk = dot3_nt(k, k)
        for h in (2 * g, 2 * g + 1):
            v = conv(512 + h * DV, DV, lambda j: taps_v[j : j + 1, h * DV : (h + 1) * DV])
            beta = col8[:, h : h + 1]
            growth = growth8[:, VH + h : VH + h + 1]
            closing = closing8[:, VH + h : VH + h + 1]
            weighted = fades(col8[:, VH + h : VH + h + 1], lower) * kk * beta
            m = jnp.concatenate([weighted[:HALF, :HALF], weighted[HALF:, HALF:]], 1)
            m = jnp.where(strict_pair, m, 0.0)
            corner = weighted[HALF:, :HALF]
            t = eye_pair - jnp.where((prow ^ pcol) == 1, m, 0.0)
            for level in range(1, 7):
                part = jnp.where(((prow >> level) ^ (pcol >> level)) == 1, m, 0.0)
                t = t - dot3_blocks(t, dot3_blocks(part, t))
            right = jnp.concatenate([k * growth, v], 1) * beta
            x1 = dot3(t[:, :HALF], right[:HALF])
            x2 = dot3(t[:, HALF:], right[HALF:] - dot3(corner, x1))
            ef = jnp.concatenate([x1, x2], 0)
            ef_out[h] = ef
            both = dot3((k * closing).T, ef)
            maps[h] = jnp.concatenate(
                [growth[SEG - 1 : SEG] * eye - both[:, :DK], both[:, DK:]], 1
            )
    mine = place[0]
    for slot, out in enumerate((out0, out1, out2, out3)):
        out[...] = maps[mine ^ slot]


def reply_kernel(q_in, k_in, ef, cols8, out):
    rows, cols = iota2((SEG, SEG), 0), iota2((SEG, SEG), 1)
    lower = lower_ones()
    col8 = cols8[...]
    dhi, dmid, dlo = split3(col8)
    growth8 = jnp.exp(mm(lower, dhi) + mm(lower, dmid) + mm(lower, dlo))
    for g in range(QKH):
        q = q_in[g]
        qk = dot3_nt(q, k_in[g])
        for h in (2 * g, 2 * g + 1):
            fade = fades(col8[:, VH + h : VH + h + 1], lower)
            mixing = jnp.where(rows >= cols, fade * qk, 0.0)
            both = dot3(mixing, ef[h])
            out[h] = jnp.concatenate(
                [q * growth8[:, VH + h : VH + h + 1] - both[:, :DK], both[:, DK:]], 1
            )


def after(second, first):
    prod = dot3(second[:, :DK], first)
    return jnp.concatenate([prod[:, :DK], prod[:, DK:] + second[:, DK:]], 1)


def quad_kernel(place, r0, r1, r2, r3, total, prefixes, maps):
    mine = place[0]
    for slot, r in enumerate((r0, r1, r2, r3)):
        maps[mine ^ slot] = r[...]
    first = maps[0]
    pair = after(maps[1], first)
    total[...] = after(after(maps[3], maps[2]), pair)
    prefixes[0] = first
    prefixes[1] = pair
    prefixes[2] = after(maps[2], pair)


def row_kernel(place, own, other, out):
    behind = place[1] == 1
    first = jnp.where(behind, other[...], own[...])
    second = jnp.where(behind, own[...], other[...])
    out[...] = after(second, first)


def state_kernel(place, y1, y2, y3, other, prefixes, out0, out1, out2, out3, states):
    s = y3[:, DK:]
    s = dot3(y2[:, :DK], s) + y2[:, DK:]
    s = dot3(y1[:, :DK], s) + y1[:, DK:]
    s = jnp.where(place[1] == 1, dot3(other[:, :DK], s) + other[:, DK:], s)
    states[0] = s
    for j in range(3):
        states[j + 1] = dot3(prefixes[j, :, :DK], s) + prefixes[j, :, DK:]
    mine = place[0]
    for slot, out in enumerate((out0, out1, out2, out3)):
        out[...] = states[mine ^ slot]


def normed_kernel(place, r0, r1, r2, r3, reply, vz, gain, w_out, normed, out, states):
    mine = place[0]
    for slot, r in enumerate((r0, r1, r2, r3)):
        states[mine ^ slot] = r[...]
    for h in range(VH):
        core = dot3(reply[h, :, :DK], states[h]) + reply[h, :, DK:]
        z = vz[1, :, h * DV : (h + 1) * DV]
        scale = lax.rsqrt(jnp.mean(core * core, -1, keepdims=True) + EPS)
        normed[:, h * DV : (h + 1) * DV] = (core * scale * gain[...] * silu(z)).astype(BF16)
    product_blocks(place[2], 1 - place[3], normed, w_out, out)


def product_blocks(x, core, normed, w_out, out):
    for r in range(4):
        start = pl.multiple_of((((x + r) & 3) * 2 + core) * 256, 256)
        out[r] = mm(normed[...], w_out[:, pl.ds(start, 256)])


def own_kernel(place, normed, w_out, out):
    product_blocks(place[2], place[3], normed, w_out, out)


def arr(*shape, dtype=F32):
    return jax.ShapeDtypeStruct(shape, dtype)


def swap(v, axis, size, mask):
    return lax.ppermute(v, axis, [(i, i ^ mask) for i in range(size)])


def shift(v, axis, size, step):
    return lax.ppermute(v, axis, [(i, (i + step) % size) for i in range(size)])


def forward(v, axis, size, step):
    return lax.ppermute(v, axis, [(i, i + step) for i in range(size - step)])


def local(tokens, w_qk, w_vz, w_ab, conv_qk, conv_v, a_log, dt_bias, beta_bias, norm_gain, w_out):
    y, z = lax.axis_index("y"), lax.axis_index("z")
    x, core = lax.axis_index("x"), lax.axis_index("core")
    place = jnp.stack([z & 3, z >> 2, x, core]).astype(jnp.int32)

    qk = jnp.einsum("td,dcf->ctf", tokens, w_qk, preferred_element_type=F32)
    vz = jnp.einsum("td,dcf->ctf", tokens, w_vz, preferred_element_type=F32)
    ab = jnp.einsum("td,dcf->cft", tokens, w_ab, preferred_element_type=F32)
    tail = jnp.concatenate([qk[0, SEG - 8 :], qk[1, SEG - 8 :], vz[0, SEG - 8 :]], 1)
    halo = lax.ppermute(tail, ("y", "z"), [(i, i + 1) for i in range(31)])

    seg = pl.pallas_call(
        segment_kernel,
        out_shape=[arr(DK, 256)] * 4
        + [arr(QKH, SEG, DK), arr(QKH, SEG, DK), arr(VH, SEG, 256), arr(SEG, 8)],
        in_specs=[SMEM] * 4 + [VMEM] * 6,
        out_specs=[VMEM] * 8,
        scratch_shapes=[pltpu.VMEM((SEG + 8, 1024), F32), pltpu.VMEM((VH, DK, 256), F32)],
        compiler_params=params(24),
        cost_estimate=pl.CostEstimate(flops=6 * 10**9, bytes_accessed=6 * 10**6, transcendentals=0),
        name="segment",
    )(place, a_log, dt_bias, beta_bias, qk, vz, halo, conv_qk, conv_v, ab)
    maps, (q, k, ef, cols8) = seg[:4], seg[4:]

    got = [maps[0]] + [swap(maps[m], "z", 8, m) for m in (1, 2, 3)]
    reply = pl.pallas_call(
        reply_kernel,
        out_shape=arr(VH, SEG, 256),
        in_specs=[VMEM] * 4,
        out_specs=VMEM,
        compiler_params=params(24),
        cost_estimate=pl.CostEstimate(flops=2 * 10**9, bytes_accessed=3 * 10**6, transcendentals=0),
        name="reply",
    )(q, k, ef, cols8)

    total, prefixes = pl.pallas_call(
        quad_kernel,
        out_shape=[arr(DK, 256), arr(3, DK, 256)],
        in_specs=[SMEM] + [VMEM] * 4,
        out_specs=[VMEM] * 2,
        scratch_shapes=[pltpu.VMEM((4, DK, 256), F32)],
        compiler_params=params(16),
        name="quad",
    )(place, *got)
    other = swap(total, "z", 8, 4)
    row = pl.pallas_call(
        row_kernel,
        out_shape=arr(DK, 256),
        in_specs=[SMEM] + [VMEM] * 2,
        out_specs=VMEM,
        compiler_params=params(16),
        name="row",
    )(place, total, other)
    rows = [forward(row, "y", 4, d) for d in (1, 2, 3)]
    states = pl.pallas_call(
        state_kernel,
        out_shape=[arr(DK, DV)] * 4,
        in_specs=[SMEM] + [VMEM] * 5,
        out_specs=[VMEM] * 4,
        scratch_shapes=[pltpu.VMEM((4, DK, DV), F32)],
        compiler_params=params(16),
        name="state",
    )(place, *rows, other, prefixes)
    came = [states[0]] + [swap(states[m], "z", 8, m) for m in (1, 2, 3)]

    normed, for_twin = pl.pallas_call(
        normed_kernel,
        out_shape=[arr(SEG, VH * DV, dtype=BF16), arr(4, SEG, 256)],
        in_specs=[SMEM] + [VMEM] * 8,
        out_specs=[VMEM] * 2,
        scratch_shapes=[pltpu.VMEM((4, DK, DV), F32)],
        compiler_params=params(24),
        name="normed",
    )(place, *came, reply, vz, norm_gain.reshape(1, DV), w_out)
    from_twin = swap(for_twin, "core", 2, 1)
    own = pl.pallas_call(
        own_kernel,
        out_shape=arr(4, SEG, 256),
        in_specs=[SMEM] + [VMEM] * 2,
        out_specs=VMEM,
        compiler_params=params(24),
        cost_estimate=pl.CostEstimate(flops=10**9, bytes_accessed=3 * 10**6, transcendentals=0),
        name="own",
    )(place, normed, w_out)

    far = own[2] + from_twin[2]
    from_left = shift(far[:HALF], "x", 4, 1)
    from_right = shift(far[HALF:], "x", 4, -1)
    chip = own + from_twin
    to_right = jnp.concatenate([chip[1, :HALF] + from_left, chip[1, HALF:]], 0)
    to_left = jnp.concatenate([chip[3, :HALF], chip[3, HALF:] + from_right], 0)
    last_left = shift(to_right, "x", 4, 1)
    last_right = shift(to_left, "x", 4, -1)
    return (chip[0] + (last_left + last_right)).astype(BF16)


def solution(mesh):
    split = Mesh(mesh.devices.reshape(4, 8, 4, 2), ("y", "z", "x", "core"))
    seq, head = ("y", "z"), ("x", "core")
    in_specs = (
        P(seq, None),
        P(None, None, head),
        P(None, None, head),
        P(None, None, head),
        P(None, None, head),
        P(None, head),
        P(head),
        P(head),
        P(head),
        P(),
        P(head, None),
    )
    return jax.shard_map(
        local, mesh=split, in_specs=in_specs, out_specs=P(seq, head), check_vma=False
    )
```

```python
import functools

import jax
import jax.numpy as jnp
from jax import lax
from jax.experimental import pallas as pl
from jax.experimental.pallas import tpu as pltpu
from jax.sharding import Mesh, PartitionSpec as P

F32 = jnp.float32
BF16 = jnp.bfloat16
DK = 128
DV = 128
HALF = 128
SEG = 256
VH = 4
QKH = 2
EPS = 1e-06
FLOOR = -110.0

VMEM = pl.BlockSpec(memory_space=pltpu.VMEM)
SMEM = pl.BlockSpec(memory_space=pltpu.SMEM)


def params(mib):
    return pltpu.CompilerParams(vmem_limit_bytes=mib * 1024 * 1024)


def split2(x):
    hi = x.astype(BF16)
    return hi, (x - hi.astype(F32)).astype(BF16)


def split3(x):
    hi = x.astype(BF16)
    rest = x - hi.astype(F32)
    mid = rest.astype(BF16)
    return hi, mid, (rest - mid.astype(F32)).astype(BF16)


def mm(a, b):
    return jnp.dot(a, b, preferred_element_type=F32)


def mm_nt(a, b):
    return lax.dot_general(a, b, (((1,), (1,)), ((), ())), preferred_element_type=F32)


def dot3(a, b):
    ah, al = split2(a)
    bh, bl = split2(b)
    return mm(jnp.concatenate([ah, al, ah], 1), jnp.concatenate([bh, bh, bl], 0))


def dot3_nt(a, b):
    ah, al = split2(a)
    bh, bl = split2(b)
    return mm_nt(jnp.concatenate([ah, al, ah], 1), jnp.concatenate([bh, bh, bl], 1))


def spread_blocks(x):
    zero = jnp.zeros((HALF, HALF), x.dtype)
    return jnp.concatenate(
        [
            jnp.concatenate([x[:, :HALF], zero], 1),
            jnp.concatenate([zero, x[:, HALF:]], 1),
        ],
        0,
    )


def dot3_blocks(a, b):
    ah, al = split2(a)
    bh, bl = split2(b)
    bh, bl = spread_blocks(bh), spread_blocks(bl)
    return mm(jnp.concatenate([ah, al, ah], 1), jnp.concatenate([bh, bh, bl], 0))


def iota2(shape, dim):
    return lax.broadcasted_iota(jnp.int32, shape, dim)


def silu(x):
    return x / (1.0 + jnp.exp(-x))


def softplus(x):
    return jnp.maximum(x, 0.0) + jnp.log1p(jnp.exp(-jnp.abs(x)))


def unit(x):
    return x * lax.rsqrt(jnp.sum(x * x, -1, keepdims=True) + EPS)


def fades(decay_col, lower):
    rows, cols = iota2((SEG, SEG), 0), iota2((SEG, SEG), 1)
    terms = jnp.where(rows > cols, jnp.broadcast_to(decay_col, (SEG, SEG)), 0.0)
    hi, mid, lo = split3(terms)
    return jnp.exp(mm(lower, hi) + mm(lower, mid) + mm(lower, lo))


def lower_ones():
    rows, cols = iota2((SEG, SEG), 0), iota2((SEG, SEG), 1)
    return jnp.where(rows >= cols, 1.0, 0.0).astype(BF16)


def conv_part(pad, taps, width):
    total = None
    for j in range(4):
        term = pad[5 + j : 5 + j + SEG, :width] * taps(j)
        total = term if total is None else total + term
    return silu(total)


def segment_kernel(
    own_group, place, a_log, dt_bias, beta_bias, tokens, halo, w_qk, w_v, taps_qk, taps_v, w_ab,
    out0, out1, q_out, k_out, ef_out, cols_out, pad, maps,
):
    mine = place[0]
    group = (mine >> 1) if own_group else 1 - (mine >> 1)
    rows, cols = iota2((SEG, SEG), 0), iota2((SEG, SEG), 1)
    tok = tokens[...]
    before = halo[...].astype(BF16)
    lanes = pl.ds(pl.multiple_of(group * DK, DK), DK)
    wide = pl.ds(pl.multiple_of(group * 256, 256), 256)
    key_lanes = pl.ds(pl.multiple_of(256 + group * DK, DK), DK)

    def pick(taps, width):
        return jnp.where(group == 1, taps[:, width : 2 * width], taps[:, :width])

    def project(w, taps, width):
        full = mm(tok, w)
        pad[0:8, :width] = mm(before, w)
        pad[8:, :width] = full
        return conv_part(pad, taps, width)

    k = unit(project(w_qk[:, key_lanes], lambda j: pick(taps_qk[j, 1:2, :], DK), DK))
    kk = dot3_nt(k, k)
    head_rows = []
    logits = [mm_nt(w_ab[c], tok) for c in (0, 1)]
    for i in range(2):
        h = group * 2 + i
        mine_beta = jnp.where(group == 1, logits[0][2 + i : 3 + i], logits[0][i : i + 1])
        head_rows.append(jax.nn.sigmoid(mine_beta + beta_bias[h]))
    for i in range(2):
        h = group * 2 + i
        mine_decay = jnp.where(group == 1, logits[1][2 + i : 3 + i], logits[1][i : i + 1])
        rate = jnp.exp(jnp.full((1, SEG), a_log[h], F32))
        head_rows.append(jnp.maximum(-rate * softplus(mine_decay + dt_bias[h]), FLOOR))
    head_rows.append(jnp.zeros((4, SEG), F32))
    col8 = jnp.concatenate(head_rows, 0).T
    cols_out[...] = col8
    lower = lower_ones()
    later = jnp.where(rows < cols, 1.0, 0.0).astype(BF16)
    dhi, dmid, dlo = split3(col8)
    growth8 = jnp.exp(mm(lower, dhi) + mm(lower, dmid) + mm(lower, dlo))
    closing8 = jnp.exp(mm(later, dhi) + mm(later, dmid) + mm(later, dlo))

    v = project(w_v[:, wide], lambda j: pick(taps_v[j : j + 1, :], 256), 256)
    prow, pcol = iota2((HALF, SEG), 0), iota2((HALF, SEG), 1) & (HALF - 1)
    strict_pair = prow > pcol
    eye_pair = jnp.where(prow == pcol, 1.0, 0.0)
    eye = jnp.where(iota2((DK, DK), 0) == iota2((DK, DK), 1), 1.0, 0.0)
    both_heads = (0, 1)
    beta = [col8[:, i : i + 1] for i in both_heads]
    growth = [growth8[:, 2 + i : 3 + i] for i in both_heads]
    closing = [closing8[:, 2 + i : 3 + i] for i in both_heads]
    weighted = [fades(col8[:, 2 + i : 3 + i], lower) * kk * beta[i] for i in both_heads]
    m = [
        jnp.where(strict_pair, jnp.concatenate([u[:HALF, :HALF], u[HALF:, HALF:]], 1), 0.0)
        for u in weighted
    ]
    corner = [u[HALF:, :HALF] for u in weighted]
    t = [eye_pair - jnp.where((prow ^ pcol) == 1, m[i], 0.0) for i in both_heads]
    for level in range(1, 7):
        keep = ((prow >> level) ^ (pcol >> level)) == 1
        part = [jnp.where(keep, m[i], 0.0) for i in both_heads]
        inner = [dot3_blocks(part[i], t[i]) for i in both_heads]
        t = [t[i] - dot3_blocks(t[i], inner[i]) for i in both_heads]
    right = [
        jnp.concatenate([k * growth[i], v[:, i * DV : (i + 1) * DV]], 1) * beta[i]
        for i in both_heads
    ]
    x1 = [dot3(t[i][:, :HALF], right[i][:HALF]) for i in both_heads]
    rest = [right[i][HALF:] - dot3(corner[i], x1[i]) for i in both_heads]
    x2 = [dot3(t[i][:, HALF:], rest[i]) for i in both_heads]
    ef = [jnp.concatenate([x1[i], x2[i]], 0) for i in both_heads]
    both = [dot3((k * closing[i]).T, ef[i]) for i in both_heads]
    for i in both_heads:
        ef_out[i] = ef[i]
        maps[i] = jnp.concatenate(
            [growth[i][SEG - 1 : SEG] * eye - both[i][:, :DK], both[i][:, DK:]], 1
        )
    out0[...] = maps[mine & 1]
    out1[...] = maps[(mine & 1) ^ 1]
    k_out[...] = k
    q_out[...] = unit(project(w_qk[:, lanes], lambda j: pick(taps_qk[j, 0:1, :], DK), DK)) * DK ** -0.5


def reply_kernel(place, tokens, w_z, gain, q_a, k_a, ef_a, cols_a, q_b, k_b, ef_b, cols_b, out, gates):
    rows, cols = iota2((SEG, SEG), 0), iota2((SEG, SEG), 1)
    lower = lower_ones()
    mine = place[0] >> 1
    z = mm(tokens[...], w_z[...])
    for h in range(VH):
        part = z[:, h * DV : (h + 1) * DV]
        gates[:, h * DV : (h + 1) * DV] = gain[...] * silu(part)
    for group, q_in, k_in, ef, cols4 in (
        (mine, q_a, k_a, ef_a, cols_a),
        (1 - mine, q_b, k_b, ef_b, cols_b),
    ):
        col8 = cols4[...]
        dhi, dmid, dlo = split3(col8)
        growth8 = jnp.exp(mm(lower, dhi) + mm(lower, dmid) + mm(lower, dlo))
        q = q_in[...]
        qk = dot3_nt(q, k_in[...])
        for i in range(2):
            fade = fades(col8[:, 2 + i : 3 + i], lower)
            mixing = jnp.where(rows >= cols, fade * qk, 0.0)
            both = dot3(mixing, ef[i])
            out[group * 2 + i] = jnp.concatenate(
                [q * growth8[:, 2 + i : 3 + i] - both[:, :DK], both[:, DK:]], 1
            )


def after(second, first):
    prod = dot3(second[:, :DK], first)
    return jnp.concatenate([prod[:, :DK], prod[:, DK:] + second[:, DK:]], 1)


def quad_kernel(place, r0, r1, r2, r3, total, prefixes, maps):
    mine = place[0]
    for slot, r in enumerate((r0, r1, r2, r3)):
        maps[mine ^ slot] = r[...]
    first = maps[0]
    pair = after(maps[1], first)
    total[...] = after(after(maps[3], maps[2]), pair)
    prefixes[0] = first
    prefixes[1] = pair
    prefixes[2] = after(maps[2], pair)


def row_kernel(place, own, other, out):
    behind = place[1] == 1
    first = jnp.where(behind, other[...], own[...])
    second = jnp.where(behind, own[...], other[...])
    out[...] = after(second, first)


def state_kernel(place, y1, y2, y3, other, prefixes, out0, out1, out2, out3, states):
    s = y3[:, DK:]
    s = dot3(y2[:, :DK], s) + y2[:, DK:]
    s = dot3(y1[:, :DK], s) + y1[:, DK:]
    s = jnp.where(place[1] == 1, dot3(other[:, :DK], s) + other[:, DK:], s)
    states[0] = s
    for j in range(3):
        states[j + 1] = dot3(prefixes[j, :, :DK], s) + prefixes[j, :, DK:]
    mine = place[0]
    for slot, out in enumerate((out0, out1, out2, out3)):
        out[...] = states[mine ^ slot]


def normed_kernel(place, r0, r1, r2, r3, reply, gates, w_out, normed, out, states):
    mine = place[0]
    for slot, r in enumerate((r0, r1, r2, r3)):
        states[mine ^ slot] = r[...]
    for h in range(VH):
        core = dot3(reply[h, :, :DK], states[h]) + reply[h, :, DK:]
        scale = lax.rsqrt(jnp.mean(core * core, -1, keepdims=True) + EPS)
        normed[:, h * DV : (h + 1) * DV] = (core * scale * gates[:, h * DV : (h + 1) * DV]).astype(BF16)
    product_blocks(place[2], 1 - place[3], normed, w_out, out)


def product_blocks(x, core, normed, w_out, out):
    for r in range(4):
        start = pl.multiple_of((((x + r) & 3) * 2 + core) * 256, 256)
        out[r] = mm(normed[...], w_out[:, pl.ds(start, 256)])


def own_kernel(place, normed, w_out, out):
    product_blocks(place[2], place[3], normed, w_out, out)


def arr(*shape, dtype=F32):
    return jax.ShapeDtypeStruct(shape, dtype)


def swap(v, axis, size, mask):
    return lax.ppermute(v, axis, [(i, i ^ mask) for i in range(size)])


def shift(v, axis, size, step):
    return lax.ppermute(v, axis, [(i, (i + step) % size) for i in range(size)])


def forward(v, axis, size, step):
    return lax.ppermute(v, axis, [(i, i + step) for i in range(size - step)])


def segment_call(own_group, *args):
    width = args[4].shape[1]
    whole = pl.BlockSpec((width, VH * DV), lambda i: (0, 0))
    return pl.pallas_call(
        functools.partial(segment_kernel, own_group),
        grid=(1,),
        out_shape=[arr(DK, 256)] * 2
        + [arr(SEG, DK), arr(SEG, DK), arr(2, SEG, 256), arr(SEG, 8)],
        in_specs=[SMEM] * 4 + [VMEM, VMEM, VMEM, whole] + [VMEM] * 3,
        out_specs=[VMEM] * 6,
        scratch_shapes=[pltpu.VMEM((SEG + 8, 256), F32), pltpu.VMEM((2, DK, 256), F32)],
        compiler_params=params(28),
        cost_estimate=pl.CostEstimate(flops=6 * 10**9, bytes_accessed=6 * 10**6, transcendentals=0),
        name="segment_own" if own_group else "segment_other",
    )(*args)


def local(tokens, w_qk, w_vz, w_ab, conv_qk, conv_v, a_log, dt_bias, beta_bias, norm_gain, w_out):
    y, z = lax.axis_index("y"), lax.axis_index("z")
    x, core = lax.axis_index("x"), lax.axis_index("core")
    place = jnp.stack([z & 3, z >> 2, x, core]).astype(jnp.int32)

    tail = tokens[SEG - 8 :].astype(F32)
    halo = lax.ppermute(tail, ("y", "z"), [(i, i + 1) for i in range(31)])
    flat_qk = w_qk.reshape(w_qk.shape[0], 2 * QKH * DK)
    flat_vz = w_vz.reshape(w_vz.shape[0], 2 * VH * DV)
    ab = w_ab.transpose(1, 2, 0)
    args = (place, a_log, dt_bias, beta_bias, tokens, halo, flat_qk, flat_vz, conv_qk, conv_v, ab)
    far = segment_call(False, *args)
    near = segment_call(True, *args)
    got = [near[0], swap(near[1], "z", 8, 1), swap(far[0], "z", 8, 2), swap(far[1], "z", 8, 3)]
    reply, gates = pl.pallas_call(
        reply_kernel,
        grid=(1,),
        out_shape=[arr(VH, SEG, 256), arr(SEG, VH * DV)],
        in_specs=[SMEM, VMEM, pl.BlockSpec((tokens.shape[1], VH * DV), lambda i: (0, 1))] + [VMEM] * 9,
        out_specs=[VMEM] * 2,
        compiler_params=params(28),
        cost_estimate=pl.CostEstimate(flops=2 * 10**9, bytes_accessed=3 * 10**6, transcendentals=0),
        name="reply",
    )(place, tokens, flat_vz, norm_gain.reshape(1, DV), *near[2:], *far[2:])

    total, prefixes = pl.pallas_call(
        quad_kernel,
        out_shape=[arr(DK, 256), arr(3, DK, 256)],
        in_specs=[SMEM] + [VMEM] * 4,
        out_specs=[VMEM] * 2,
        scratch_shapes=[pltpu.VMEM((4, DK, 256), F32)],
        compiler_params=params(16),
        name="quad",
    )(place, *got)
    other = swap(total, "z", 8, 4)
    row = pl.pallas_call(
        row_kernel,
        out_shape=arr(DK, 256),
        in_specs=[SMEM] + [VMEM] * 2,
        out_specs=VMEM,
        compiler_params=params(16),
        name="row",
    )(place, total, other)
    rows = [forward(row, "y", 4, d) for d in (1, 2, 3)]
    states = pl.pallas_call(
        state_kernel,
        out_shape=[arr(DK, DV)] * 4,
        in_specs=[SMEM] + [VMEM] * 5,
        out_specs=[VMEM] * 4,
        scratch_shapes=[pltpu.VMEM((4, DK, DV), F32)],
        compiler_params=params(16),
        name="state",
    )(place, *rows, other, prefixes)
    came = [states[0]] + [swap(states[m], "z", 8, m) for m in (1, 2, 3)]

    normed, for_twin = pl.pallas_call(
        normed_kernel,
        out_shape=[arr(SEG, VH * DV, dtype=BF16), arr(4, SEG, 256)],
        in_specs=[SMEM] + [VMEM] * 7,
        out_specs=[VMEM] * 2,
        scratch_shapes=[pltpu.VMEM((4, DK, DV), F32)],
        compiler_params=params(24),
        name="normed",
    )(place, *came, reply, gates, w_out)
    from_twin = swap(for_twin, "core", 2, 1)
    own = pl.pallas_call(
        own_kernel,
        out_shape=arr(4, SEG, 256),
        in_specs=[SMEM] + [VMEM] * 2,
        out_specs=VMEM,
        compiler_params=params(24),
        cost_estimate=pl.CostEstimate(flops=10**9, bytes_accessed=3 * 10**6, transcendentals=0),
        name="own",
    )(place, normed, w_out)

    across = own[2] + from_twin[2]
    from_left = shift(across[:HALF], "x", 4, 1)
    from_right = shift(across[HALF:], "x", 4, -1)
    chip = own + from_twin
    to_right = jnp.concatenate([chip[1, :HALF] + from_left, chip[1, HALF:]], 0)
    to_left = jnp.concatenate([chip[3, :HALF], chip[3, HALF:] + from_right], 0)
    last_left = shift(to_right, "x", 4, 1)
    last_right = shift(to_left, "x", 4, -1)
    return (chip[0] + (last_left + last_right)).astype(BF16)


def solution(mesh):
    split = Mesh(mesh.devices.reshape(4, 8, 4, 2), ("y", "z", "x", "core"))
    seq, head = ("y", "z"), ("x", "core")
    in_specs = (
        P(seq, None),
        P(None, None, head),
        P(None, None, head),
        P(None, None, head),
        P(None, None, head),
        P(None, head),
        P(head),
        P(head),
        P(head),
        P(),
        P(head, None),
    )
    return jax.shard_map(
        local, mesh=split, in_specs=in_specs, out_specs=P(seq, head), check_vma=False
    )
```

```python
import functools

import jax
import jax.numpy as jnp
from jax import lax
from jax.experimental import pallas as pl
from jax.experimental.pallas import tpu as pltpu
from jax.sharding import Mesh, PartitionSpec as P

F32 = jnp.float32
BF16 = jnp.bfloat16
DK = 128
DV = 128
HALF = 128
SEG = 256
VH = 4
QKH = 2
EPS = 1e-06
FLOOR = -110.0

VMEM = pl.BlockSpec(memory_space=pltpu.VMEM)
SMEM = pl.BlockSpec(memory_space=pltpu.SMEM)


def params(mib):
    return pltpu.CompilerParams(vmem_limit_bytes=mib * 1024 * 1024)


def split2(x):
    hi = x.astype(BF16)
    return hi, (x - hi.astype(F32)).astype(BF16)


def split3(x):
    hi = x.astype(BF16)
    rest = x - hi.astype(F32)
    mid = rest.astype(BF16)
    return hi, mid, (rest - mid.astype(F32)).astype(BF16)


def mm(a, b):
    return jnp.dot(a, b, preferred_element_type=F32)


def mm_nt(a, b):
    return lax.dot_general(a, b, (((1,), (1,)), ((), ())), preferred_element_type=F32)


def dot3(a, b):
    ah, al = split2(a)
    bh, bl = split2(b)
    return mm(jnp.concatenate([ah, al, ah], 1), jnp.concatenate([bh, bh, bl], 0))


def dot3_nt(a, b):
    ah, al = split2(a)
    bh, bl = split2(b)
    return mm_nt(jnp.concatenate([ah, al, ah], 1), jnp.concatenate([bh, bh, bl], 1))


def spread_blocks(x):
    zero = jnp.zeros((HALF, HALF), x.dtype)
    return jnp.concatenate(
        [
            jnp.concatenate([x[:, :HALF], zero], 1),
            jnp.concatenate([zero, x[:, HALF:]], 1),
        ],
        0,
    )


def dot3_blocks(a, b):
    ah, al = split2(a)
    bh, bl = split2(b)
    bh, bl = spread_blocks(bh), spread_blocks(bl)
    return mm(jnp.concatenate([ah, al, ah], 1), jnp.concatenate([bh, bh, bl], 0))


def iota2(shape, dim):
    return lax.broadcasted_iota(jnp.int32, shape, dim)


def silu(x):
    return x / (1.0 + jnp.exp(-x))


def softplus(x):
    return jnp.maximum(x, 0.0) + jnp.log1p(jnp.exp(-jnp.abs(x)))


def unit(x):
    return x * lax.rsqrt(jnp.sum(x * x, -1, keepdims=True) + EPS)


def fades(decay_col, lower):
    rows, cols = iota2((SEG, SEG), 0), iota2((SEG, SEG), 1)
    terms = jnp.where(rows > cols, jnp.broadcast_to(decay_col, (SEG, SEG)), 0.0)
    hi, mid, lo = split3(terms)
    return jnp.exp(mm(lower, hi) + mm(lower, mid) + mm(lower, lo))


def lower_ones():
    rows, cols = iota2((SEG, SEG), 0), iota2((SEG, SEG), 1)
    return jnp.where(rows >= cols, 1.0, 0.0).astype(BF16)


def dot3_parts(ah, al, bh, bl):
    return mm(jnp.concatenate([ah, al, ah], 1), jnp.concatenate([bh, bh, bl], 0))


def conv(pad, block, tap):
    total = None
    for j in range(4):
        term = pad[block, 5 + j : 5 + j + SEG, :] * tap(j)
        total = term if total is None else total + term
    return silu(total)


def project(pad, tok, before, w, block, count):
    full, front = mm(tok, w), mm(before, w)
    for i in range(count):
        pad[block + i, 0:8, :] = front[:, i * 128 : (i + 1) * 128]
        pad[block + i, 8:, :] = full[:, i * 128 : (i + 1) * 128]


def sums_of(parts, weights):
    return jnp.exp(sum(mm(weights, part) for part in parts))


def affine_maps(keys, grams, values, col8, slots):
    rows, cols = iota2((SEG, SEG), 0), iota2((SEG, SEG), 1)
    lower = lower_ones()
    later = jnp.where(rows < cols, 1.0, 0.0).astype(BF16)
    parts = split3(col8)
    growth8, closing8 = sums_of(parts, lower), sums_of(parts, later)
    n = range(len(slots))
    beta = [col8[:, c : c + 1] for c in slots]
    growth = [growth8[:, 4 + c : 5 + c] for c in slots]
    closing = [closing8[:, 4 + c : 5 + c] for c in slots]
    prow, pcol = iota2((HALF, HALF), 0), iota2((HALF, HALF), 1)
    strict = prow > pcol
    eye = jnp.where(prow == pcol, 1.0, 0.0)
    m, corner = [], []
    for i in n:
        u = fades(col8[:, 4 + slots[i] : 5 + slots[i]], lower) * grams[i] * beta[i]
        m += [
            jnp.where(strict, u[:HALF, :HALF], 0.0),
            jnp.where(strict, u[HALF:, HALF:], 0.0),
        ]
        corner.append(u[HALF:, :HALF])
    def within(low, high):
        return ((prow >> high) == (pcol >> high)) & ((prow >> low) != (pcol >> low))

    def mul(a, b):
        return [dot3_parts(*p, *q) for p, q in zip(a, b)]

    def halves(a):
        return [split2(u) for u in a]

    def finish(inv, power):
        square = halves(mul(power, power))
        inv = [u + w for u, w in zip(inv, mul(square, halves(inv)))]
        fourth = halves(mul(square, square))
        return [u + w for u, w in zip(inv, mul(fourth, halves(inv)))]

    near_diag = [jnp.where(within(0, 3), u, 0.0) for u in m]
    t = finish([eye - u for u in near_diag], halves(near_diag))
    ts = halves(t)
    power = halves(mul(ts, halves([jnp.where(within(3, 6), u, 0.0) for u in m])))
    t = finish([u - w for u, w in zip(t, mul(power, ts))], power)
    ts = halves(t)
    inner = halves(mul(halves([jnp.where(within(6, 7), u, 0.0) for u in m]), ts))
    t = [u - w for u, w in zip(t, mul(ts, inner))]
    right = [jnp.concatenate([keys[i] * growth[i], values[i]], 1) * beta[i] for i in n]
    x1 = [dot3(t[2 * i], right[i][:HALF]) for i in n]
    later_half = [dot3(t[2 * i + 1], right[i][HALF:]) for i in n]
    carry = [dot3(t[2 * i + 1], corner[i]) for i in n]
    x2 = [later_half[i] - dot3(carry[i], x1[i]) for i in n]
    ef = [jnp.concatenate([x1[i], x2[i]], 0) for i in n]
    both = [dot3((keys[i] * closing[i]).T, ef[i]) for i in n]
    maps = [
        jnp.concatenate([growth[i][SEG - 1 : SEG] * eye - both[i][:, :DK], both[i][:, DK:]], 1)
        for i in n
    ]
    return maps, ef


def segment_kernel(
    own_group, place, a_log, dt_bias, beta_bias, tokens, halo, w_qk, w_v, taps_qk, taps_v, w_ab,
    out0, out1, k_out, ef_out, cols_out, pad, logits, values,
):
    mine = place[0]
    group = (mine >> 1) if own_group else 1 - (mine >> 1)
    tok = tokens[...]
    before = halo[...].astype(BF16)
    wide = pl.ds(pl.multiple_of(group * 256, 256), 256)
    key_lanes = pl.ds(pl.multiple_of(256 + group * DK, DK), DK)

    def pick(taps, width):
        return jnp.where(group == 1, taps[:, width : 2 * width], taps[:, :width])

    logits[...] = mm_nt(tok, jnp.concatenate([w_ab[0], w_ab[1]], 0)).T
    project(pad, tok, before, w_qk[:, key_lanes], 0, 1)
    project(pad, tok, before, w_v[:, wide], 1, 2)
    betas, decays = [], []
    for slot in range(2):
        h = group * 2 + ((mine & 1) ^ slot)
        betas.append(jax.nn.sigmoid(logits[pl.ds(h, 1), :] + beta_bias[h]))
        rate = jnp.exp(jnp.full((1, SEG), a_log[h], F32))
        decay = -rate * softplus(logits[pl.ds(h + 4, 1), :] + dt_bias[h])
        decays.append(jnp.maximum(decay, FLOOR))
    blank = jnp.zeros((2, SEG), F32)
    col8 = jnp.concatenate(betas + [blank] + decays + [blank], 0).T
    cols_out[...] = col8
    k = unit(conv(pad, 0, lambda j: pick(taps_qk[j, 1:2, :], DK)))
    k_out[...] = k
    gram = dot3_nt(k, k)
    for i in range(2):
        values[i] = conv(
            pad, 1 + i, lambda j: pick(taps_v[j : j + 1, :], 256)[:, i * DV : (i + 1) * DV]
        )
    maps, ef = affine_maps(
        [k, k], [gram, gram], [values[(mine & 1) ^ i] for i in range(2)], col8, (0, 1)
    )
    for i, out in enumerate((out0, out1)):
        out[...] = maps[i]
        ef_out[i] = ef[i]


def reply_kernel(
    place, tokens, halo, w_q, w_z, taps_qk, gain, k_near, ef_near, cols_near, k_far, ef_far, cols_far,
    out, gates, pad, queries,
):
    rows, cols = iota2((SEG, SEG), 0), iota2((SEG, SEG), 1)
    lower = lower_ones()
    mine = place[0]
    tok = tokens[...]
    project(pad, tok, halo[...].astype(BF16), w_q[...], 0, 2)
    z = mm(tok, w_z[...])
    for h in range(VH):
        part = z[:, h * DV : (h + 1) * DV]
        gates[:, h * DV : (h + 1) * DV] = gain[...] * silu(part)
    for g in range(QKH):
        taps = lambda j: taps_qk[j, 0:1, g * DK : (g + 1) * DK]
        queries[g] = unit(conv(pad, g, taps)) * DK ** -0.5
    for side, k, ef, cols8 in ((0, k_near, ef_near, cols_near), (1, k_far, ef_far, cols_far)):
        q = queries[(mine >> 1) ^ side]
        col8 = cols8[...]
        growth8 = sums_of(split3(col8), lower)
        qk = dot3_nt(q, k[...])
        for i in range(2):
            fade = fades(col8[:, 4 + i : 5 + i], lower)
            mixing = jnp.where(rows >= cols, fade * qk, 0.0)
            both = dot3(mixing, ef[i])
            out[mine ^ (2 * side + i)] = jnp.concatenate(
                [q * growth8[:, 4 + i : 5 + i] - both[:, :DK], both[:, DK:]], 1
            )


def after(second, first):
    prod = dot3(second[:, :DK], first)
    return jnp.concatenate([prod[:, :DK], prod[:, DK:] + second[:, DK:]], 1)


def pair_kernel(place, r2, r3, out):
    odd = (place[0] & 1) == 1
    out[...] = after(
        jnp.where(odd, r2[...], r3[...]), jnp.where(odd, r3[...], r2[...])
    )


def quad_kernel(place, r0, r1, r2, r3, far, total, prefixes):
    odd, upper = (place[0] & 1) == 1, place[0] >= 2
    near_first = jnp.where(odd, r1[...], r0[...])
    near_second = jnp.where(odd, r0[...], r1[...])
    near = after(near_second, near_first)
    far_first = jnp.where(odd, r3[...], r2[...])
    first, second = jnp.where(upper, far[...], near), jnp.where(upper, near, far[...])
    total[...] = after(second, first)
    prefixes[0] = jnp.where(upper, far_first, near_first)
    prefixes[1] = first
    prefixes[2] = after(jnp.where(upper, near_first, far_first), first)


def row_kernel(place, own, other, out):
    behind = place[1] == 1
    first = jnp.where(behind, other[...], own[...])
    second = jnp.where(behind, own[...], other[...])
    out[...] = after(second, first)


def early_kernel(y2, y3, out):
    out[...] = dot3(y2[:, :DK], y3[:, DK:]) + y2[:, DK:]


def state_kernel(place, y1, early, other, prefixes, out0, out1, out2, out3, states):
    s = dot3(y1[:, :DK], early[...]) + y1[:, DK:]
    s = jnp.where(place[1] == 1, dot3(other[:, :DK], s) + other[:, DK:], s)
    states[0] = s
    for j in range(3):
        states[j + 1] = dot3(prefixes[j, :, :DK], s) + prefixes[j, :, DK:]
    mine = place[0]
    for slot, out in enumerate((out0, out1, out2, out3)):
        out[...] = states[mine ^ slot]


def normed_kernel(place, r0, r1, r2, r3, reply, gates, w_out, normed, out, states):
    mine = place[0]
    for slot, r in enumerate((r0, r1, r2, r3)):
        states[mine ^ slot] = r[...]
    for h in range(VH):
        core = dot3(reply[h, :, :DK], states[h]) + reply[h, :, DK:]
        scale = lax.rsqrt(jnp.mean(core * core, -1, keepdims=True) + EPS)
        normed[:, h * DV : (h + 1) * DV] = (core * scale * gates[:, h * DV : (h + 1) * DV]).astype(BF16)
    for step in range(4):
        out[step] = block_product(normed, w_out, place, step, 1 - place[3])


def block_product(normed, w_out, place, step, core):
    start = pl.multiple_of((((place[2] + step) & 3) * 2 + core) * 256, 256)
    return mm(normed[...], w_out[:, pl.ds(start, 256)])


def own_kernel(place, normed, w_out, own):
    for step in range(4):
        own[step] = block_product(normed, w_out, place, step, place[3])


def arr(*shape, dtype=F32):
    return jax.ShapeDtypeStruct(shape, dtype)


def swap(v, axis, size, mask):
    return lax.ppermute(v, axis, [(i, i ^ mask) for i in range(size)])


def shift(v, axis, size, step):
    return lax.ppermute(v, axis, [(i, (i + step) % size) for i in range(size)])


def forward(v, axis, size, step):
    return lax.ppermute(v, axis, [(i, i + step) for i in range(size - step)])


def local(tokens, w_qk, w_vz, w_ab, conv_qk, conv_v, a_log, dt_bias, beta_bias, norm_gain, w_out):
    y, z = lax.axis_index("y"), lax.axis_index("z")
    x, core = lax.axis_index("x"), lax.axis_index("core")
    place = jnp.stack([z & 3, z >> 2, x, core]).astype(jnp.int32)

    tail = tokens[SEG - 8 :].astype(F32)
    halo = lax.ppermute(tail, ("y", "z"), [(i, i + 1) for i in range(31)])
    flat_qk = w_qk.reshape(w_qk.shape[0], 2 * QKH * DK)
    flat_vz = w_vz.reshape(w_vz.shape[0], 2 * VH * DV)
    ab = w_ab.transpose(1, 2, 0)
    width = tokens.shape[1]
    half_of = lambda size, c: pl.BlockSpec((width, size), lambda i: (0, c))

    def segment(own_group):
        return pl.pallas_call(
            functools.partial(segment_kernel, own_group),
            grid=(1,),
            out_shape=[arr(DK, 256)] * 2 + [arr(SEG, DK), arr(2, SEG, 256), arr(SEG, 8)],
            in_specs=[SMEM] * 4 + [VMEM, VMEM, VMEM, half_of(VH * DV, 0)] + [VMEM] * 3,
            out_specs=[VMEM] * 5,
            scratch_shapes=[
                pltpu.VMEM((3, SEG + 8, DK), F32),
                pltpu.VMEM((8, SEG), F32),
                pltpu.VMEM((2, SEG, DV), F32),
            ],
            compiler_params=params(28),
            cost_estimate=pl.CostEstimate(
                flops=6 * 10**9, bytes_accessed=6 * 10**6, transcendentals=0
            ),
            name="segment_own" if own_group else "segment_other",
        )(place, a_log, dt_bias, beta_bias, tokens, halo, flat_qk, flat_vz, conv_qk, conv_v, ab)

    far = segment(False)
    near = segment(True)
    got = [near[0], swap(near[1], "z", 8, 1), swap(far[0], "z", 8, 2), swap(far[1], "z", 8, 3)]
    reply, gates = pl.pallas_call(
        reply_kernel,
        grid=(1,),
        out_shape=[arr(VH, SEG, 256), arr(SEG, VH * DV)],
        in_specs=[SMEM, VMEM, VMEM, half_of(QKH * DK, 0), half_of(VH * DV, 1)] + [VMEM] * 8,
        out_specs=[VMEM] * 2,
        scratch_shapes=[pltpu.VMEM((2, SEG + 8, DK), F32), pltpu.VMEM((QKH, SEG, DK), F32)],
        compiler_params=params(28),
        cost_estimate=pl.CostEstimate(flops=4 * 10**9, bytes_accessed=3 * 10**6, transcendentals=0),
        name="reply",
    )(place, tokens, halo, flat_qk, flat_vz, conv_qk, norm_gain.reshape(1, DV), *near[2:], *far[2:])

    far_pair = pl.pallas_call(
        pair_kernel,
        out_shape=arr(DK, 256),
        in_specs=[SMEM] + [VMEM] * 2,
        out_specs=VMEM,
        compiler_params=params(16),
        name="pair",
    )(place, *got[2:])
    total, prefixes = pl.pallas_call(
        quad_kernel,
        out_shape=[arr(DK, 256), arr(3, DK, 256)],
        in_specs=[SMEM] + [VMEM] * 5,
        out_specs=[VMEM] * 2,
        compiler_params=params(16),
        name="quad",
    )(place, *got, far_pair)
    other = swap(total, "z", 8, 4)
    row = pl.pallas_call(
        row_kernel,
        out_shape=arr(DK, 256),
        in_specs=[SMEM] + [VMEM] * 2,
        out_specs=VMEM,
        compiler_params=params(16),
        name="row",
    )(place, total, other)
    rows = [forward(row, "y", 4, d) for d in (1, 2, 3)]
    early = pl.pallas_call(
        early_kernel,
        out_shape=arr(DK, DV),
        in_specs=[VMEM] * 2,
        out_specs=VMEM,
        compiler_params=params(16),
        name="early",
    )(*rows[1:])
    states = pl.pallas_call(
        state_kernel,
        out_shape=[arr(DK, DV)] * 4,
        in_specs=[SMEM] + [VMEM] * 4,
        out_specs=[VMEM] * 4,
        scratch_shapes=[pltpu.VMEM((4, DK, DV), F32)],
        compiler_params=params(16),
        name="state",
    )(place, rows[0], early, other, prefixes)
    came = [states[0]] + [swap(states[m], "z", 8, m) for m in (1, 2, 3)]

    normed, for_twin = pl.pallas_call(
        normed_kernel,
        out_shape=[arr(SEG, VH * DV, dtype=BF16), arr(4, SEG, 256)],
        in_specs=[SMEM] + [VMEM] * 7,
        out_specs=[VMEM] * 2,
        scratch_shapes=[pltpu.VMEM((4, DK, DV), F32)],
        compiler_params=params(24),
        name="normed",
    )(place, *came, reply, gates, w_out)
    from_twin = swap(for_twin, "core", 2, 1)
    own = pl.pallas_call(
        own_kernel,
        out_shape=arr(4, SEG, 256),
        in_specs=[SMEM] + [VMEM] * 2,
        out_specs=VMEM,
        compiler_params=params(24),
        cost_estimate=pl.CostEstimate(flops=10**9, bytes_accessed=3 * 10**6, transcendentals=0),
        name="own",
    )(place, normed, w_out)

    from_left = shift(own[2, :HALF] + from_twin[2, :HALF], "x", 4, 1)
    from_right = shift(own[2, HALF:] + from_twin[2, HALF:], "x", 4, -1)
    right = own[1] + from_twin[1]
    left = own[3] + from_twin[3]
    to_right = jnp.concatenate([right[:HALF] + from_left, right[HALF:]], 0)
    to_left = jnp.concatenate([left[:HALF], left[HALF:] + from_right], 0)
    last_left = shift(to_right, "x", 4, 1)
    last_right = shift(to_left, "x", 4, -1)
    return ((own[0] + from_twin[0]) + (last_left + last_right)).astype(BF16)


def solution(mesh):
    split = Mesh(mesh.devices.reshape(4, 8, 4, 2), ("y", "z", "x", "core"))
    seq, head = ("y", "z"), ("x", "core")
    in_specs = (
        P(seq, None),
        P(None, None, head),
        P(None, None, head),
        P(None, None, head),
        P(None, None, head),
        P(None, head),
        P(head),
        P(head),
        P(head),
        P(),
        P(head, None),
    )
    return jax.shard_map(
        local, mesh=split, in_specs=in_specs, out_specs=P(seq, head), check_vma=False
    )
```

```python
import functools

import jax
import jax.numpy as jnp
from jax import lax
from jax.experimental import pallas as pl
from jax.experimental.pallas import tpu as pltpu
from jax.sharding import Mesh, PartitionSpec as P

F32 = jnp.float32
BF16 = jnp.bfloat16
DK = 128
DV = 128
HALF = 128
SEG = 256
VH = 4
QKH = 2
EPS = 1e-06
FLOOR = -110.0

VMEM = pl.BlockSpec(memory_space=pltpu.VMEM)
SMEM = pl.BlockSpec(memory_space=pltpu.SMEM)


def params(mib):
    return pltpu.CompilerParams(vmem_limit_bytes=mib * 1024 * 1024)


def split2(x):
    hi = x.astype(BF16)
    return hi, (x - hi.astype(F32)).astype(BF16)


def split3(x):
    hi = x.astype(BF16)
    rest = x - hi.astype(F32)
    mid = rest.astype(BF16)
    return hi, mid, (rest - mid.astype(F32)).astype(BF16)


def mm(a, b):
    return jnp.dot(a, b, preferred_element_type=F32)


def mm_nt(a, b):
    return lax.dot_general(a, b, (((1,), (1,)), ((), ())), preferred_element_type=F32)


def dot3(a, b):
    ah, al = split2(a)
    bh, bl = split2(b)
    return mm(jnp.concatenate([ah, al, ah], 1), jnp.concatenate([bh, bh, bl], 0))


def dot3_nt(a, b):
    ah, al = split2(a)
    bh, bl = split2(b)
    return mm_nt(jnp.concatenate([ah, al, ah], 1), jnp.concatenate([bh, bh, bl], 1))


def spread_blocks(x):
    zero = jnp.zeros((HALF, HALF), x.dtype)
    return jnp.concatenate(
        [
            jnp.concatenate([x[:, :HALF], zero], 1),
            jnp.concatenate([zero, x[:, HALF:]], 1),
        ],
        0,
    )


def dot3_blocks(a, b):
    ah, al = split2(a)
    bh, bl = split2(b)
    bh, bl = spread_blocks(bh), spread_blocks(bl)
    return mm(jnp.concatenate([ah, al, ah], 1), jnp.concatenate([bh, bh, bl], 0))


def iota2(shape, dim):
    return lax.broadcasted_iota(jnp.int32, shape, dim)


def silu(x):
    return x / (1.0 + jnp.exp(-x))


def softplus(x):
    return jnp.maximum(x, 0.0) + jnp.log1p(jnp.exp(-jnp.abs(x)))


def unit(x):
    return x * lax.rsqrt(jnp.sum(x * x, -1, keepdims=True) + EPS)


def fades(decay_col, lower):
    rows, cols = iota2((SEG, SEG), 0), iota2((SEG, SEG), 1)
    terms = jnp.where(rows > cols, jnp.broadcast_to(decay_col, (SEG, SEG)), 0.0)
    hi, mid, lo = split3(terms)
    return jnp.exp(mm(lower, hi) + mm(lower, mid) + mm(lower, lo))


def lower_ones():
    rows, cols = iota2((SEG, SEG), 0), iota2((SEG, SEG), 1)
    return jnp.where(rows >= cols, 1.0, 0.0).astype(BF16)


def dot3_parts(ah, al, bh, bl):
    return mm(jnp.concatenate([ah, al, ah], 1), jnp.concatenate([bh, bh, bl], 0))


def halo_rows(halo):
    return jnp.concatenate([jnp.zeros((4, halo.shape[1]), F32), halo[...]], 0).astype(BF16)


def conv(pad, block, tap):
    total = None
    for j in range(4):
        term = pad[block, 5 + j : 5 + j + SEG, :] * tap(j)
        total = term if total is None else total + term
    return silu(total)


def project(pad, tok, before, w, block, count):
    full, front = mm(tok, w), mm(before, w)
    for i in range(count):
        pad[block + i, 0:8, :] = front[:, i * 128 : (i + 1) * 128]
        pad[block + i, 8:, :] = full[:, i * 128 : (i + 1) * 128]


def sums_of(parts, weights):
    return jnp.exp(sum(mm(weights, part) for part in parts))


def affine_maps(keys, grams, values, col8, slots):
    rows, cols = iota2((SEG, SEG), 0), iota2((SEG, SEG), 1)
    lower = lower_ones()
    later = jnp.where(rows < cols, 1.0, 0.0).astype(BF16)
    parts = split3(col8)
    growth8, closing8 = sums_of(parts, lower), sums_of(parts, later)
    n = range(len(slots))
    beta = [col8[:, c : c + 1] for c in slots]
    growth = [growth8[:, 4 + c : 5 + c] for c in slots]
    closing = [closing8[:, 4 + c : 5 + c] for c in slots]
    prow, pcol = iota2((HALF, HALF), 0), iota2((HALF, HALF), 1)
    strict = prow > pcol
    eye = jnp.where(prow == pcol, 1.0, 0.0)
    m, corner = [], []
    for i in n:
        u = fades(col8[:, 4 + slots[i] : 5 + slots[i]], lower) * grams[i] * beta[i]
        m += [
            jnp.where(strict, u[:HALF, :HALF], 0.0),
            jnp.where(strict, u[HALF:, HALF:], 0.0),
        ]
        corner.append(u[HALF:, :HALF])
    def within(low, high):
        return ((prow >> high) == (pcol >> high)) & ((prow >> low) != (pcol >> low))

    def mul(a, b):
        return [dot3_parts(*p, *q) for p, q in zip(a, b)]

    def halves(a):
        return [split2(u) for u in a]

    def finish(inv, power):
        square = halves(mul(power, power))
        inv = [u + w for u, w in zip(inv, mul(square, halves(inv)))]
        fourth = halves(mul(square, square))
        return [u + w for u, w in zip(inv, mul(fourth, halves(inv)))]

    near_diag = [jnp.where(within(0, 3), u, 0.0) for u in m]
    t = finish([eye - u for u in near_diag], halves(near_diag))
    ts = halves(t)
    power = halves(mul(ts, halves([jnp.where(within(3, 6), u, 0.0) for u in m])))
    t = finish([u - w for u, w in zip(t, mul(power, ts))], power)
    ts = halves(t)
    inner = halves(mul(halves([jnp.where(within(6, 7), u, 0.0) for u in m]), ts))
    t = [u - w for u, w in zip(t, mul(ts, inner))]
    right = [jnp.concatenate([keys[i] * growth[i], values[i]], 1) * beta[i] for i in n]
    x1 = [dot3(t[2 * i], right[i][:HALF]) for i in n]
    later_half = [dot3(t[2 * i + 1], right[i][HALF:]) for i in n]
    carry = [dot3(t[2 * i + 1], corner[i]) for i in n]
    x2 = [later_half[i] - dot3(carry[i], x1[i]) for i in n]
    ef = [jnp.concatenate([x1[i], x2[i]], 0) for i in n]
    both = [dot3((keys[i] * closing[i]).T, ef[i]) for i in n]
    maps = [
        jnp.concatenate([growth[i][SEG - 1 : SEG] * eye - both[i][:, :DK], both[i][:, DK:]], 1)
        for i in n
    ]
    return maps, ef


def segment_kernel(
    own_group, place, a_log, dt_bias, beta_bias, tokens, halo, w_qk, w_v, taps_qk, taps_v, w_ab,
    out0, out1, k_out, ef_out, cols_out, pad, logits, values,
):
    mine = place[0]
    group = (mine >> 1) if own_group else 1 - (mine >> 1)
    tok = tokens[...]
    before = halo_rows(halo)
    wide = pl.ds(pl.multiple_of(group * 256, 256), 256)
    key_lanes = pl.ds(pl.multiple_of(256 + group * DK, DK), DK)

    def pick(taps, width):
        return jnp.where(group == 1, taps[:, width : 2 * width], taps[:, :width])

    logits[...] = mm_nt(tok, jnp.concatenate([w_ab[0], w_ab[1]], 0)).T
    project(pad, tok, before, w_qk[:, key_lanes], 0, 1)
    project(pad, tok, before, w_v[:, wide], 1, 2)
    betas, decays = [], []
    for slot in range(2):
        h = group * 2 + ((mine & 1) ^ slot)
        betas.append(jax.nn.sigmoid(logits[pl.ds(h, 1), :] + beta_bias[h]))
        rate = jnp.exp(jnp.full((1, SEG), a_log[h], F32))
        decay = -rate * softplus(logits[pl.ds(h + 4, 1), :] + dt_bias[h])
        decays.append(jnp.maximum(decay, FLOOR))
    blank = jnp.zeros((2, SEG), F32)
    col8 = jnp.concatenate(betas + [blank] + decays + [blank], 0).T
    cols_out[...] = col8
    k = unit(conv(pad, 0, lambda j: pick(taps_qk[j, 1:2, :], DK)))
    k_out[...] = k
    gram = dot3_nt(k, k)
    for i in range(2):
        values[i] = conv(
            pad, 1 + i, lambda j: pick(taps_v[j : j + 1, :], 256)[:, i * DV : (i + 1) * DV]
        )
    maps, ef = affine_maps(
        [k, k], [gram, gram], [values[(mine & 1) ^ i] for i in range(2)], col8, (0, 1)
    )
    for i, out in enumerate((out0, out1)):
        out[...] = maps[i]
        ef_out[i] = ef[i]


def reply_kernel(
    place, tokens, halo, w_q, w_z, taps_qk, gain, k_near, ef_near, cols_near, k_far, ef_far, cols_far,
    out, gates, pad, queries,
):
    rows, cols = iota2((SEG, SEG), 0), iota2((SEG, SEG), 1)
    lower = lower_ones()
    mine = place[0]
    tok = tokens[...]
    project(pad, tok, halo_rows(halo), w_q[...], 0, 2)
    z = mm(tok, w_z[...])
    for h in range(VH):
        part = z[:, h * DV : (h + 1) * DV]
        gates[:, h * DV : (h + 1) * DV] = gain[...] * silu(part)
    for g in range(QKH):
        taps = lambda j: taps_qk[j, 0:1, g * DK : (g + 1) * DK]
        queries[g] = unit(conv(pad, g, taps)) * DK ** -0.5
    for side, k, ef, cols8 in ((0, k_near, ef_near, cols_near), (1, k_far, ef_far, cols_far)):
        q = queries[(mine >> 1) ^ side]
        col8 = cols8[...]
        growth8 = sums_of(split3(col8), lower)
        qk = dot3_nt(q, k[...])
        for i in range(2):
            fade = fades(col8[:, 4 + i : 5 + i], lower)
            mixing = jnp.where(rows >= cols, fade * qk, 0.0)
            both = dot3(mixing, ef[i])
            out[mine ^ (2 * side + i)] = jnp.concatenate(
                [q * growth8[:, 4 + i : 5 + i] - both[:, :DK], both[:, DK:]], 1
            )


def after(second, first):
    prod = dot3(second[:, :DK], first)
    return jnp.concatenate([prod[:, :DK], prod[:, DK:] + second[:, DK:]], 1)


def pair_kernel(place, r2, r3, out):
    odd = (place[0] & 1) == 1
    out[...] = after(
        jnp.where(odd, r2[...], r3[...]), jnp.where(odd, r3[...], r2[...])
    )


def quad_kernel(place, r0, r1, far, total, first_pair):
    odd, upper = (place[0] & 1) == 1, place[0] >= 2
    near = after(jnp.where(odd, r0[...], r1[...]), jnp.where(odd, r1[...], r0[...]))
    first, second = jnp.where(upper, far[...], near), jnp.where(upper, near, far[...])
    total[...] = after(second, first)
    first_pair[...] = first


def prefix_kernel(place, r0, r1, r2, r3, first_pair, prefixes):
    odd, upper = (place[0] & 1) == 1, place[0] >= 2
    near_first = jnp.where(odd, r1[...], r0[...])
    far_first = jnp.where(odd, r3[...], r2[...])
    prefixes[0] = jnp.where(upper, far_first, near_first)
    prefixes[1] = first_pair[...]
    prefixes[2] = after(jnp.where(upper, near_first, far_first), first_pair[...])


def row_kernel(place, own, other, after_reply, after_prefixes, out):
    behind = place[1] == 1
    first = jnp.where(behind, other[...], own[...])
    second = jnp.where(behind, own[...], other[...])
    out[...] = after(second, first)


def early_kernel(y2, y3, out):
    out[...] = dot3(y2[:, :DK], y3[:, DK:]) + y2[:, DK:]


def state_kernel(place, y1, early, other, prefixes, out0, out1, out2, out3, states):
    s = dot3(y1[:, :DK], early[...]) + y1[:, DK:]
    s = jnp.where(place[1] == 1, dot3(other[:, :DK], s) + other[:, DK:], s)
    states[0] = s
    for j in range(3):
        states[j + 1] = dot3(prefixes[j, :, :DK], s) + prefixes[j, :, DK:]
    mine = place[0]
    for slot, out in enumerate((out0, out1, out2, out3)):
        out[...] = states[mine ^ slot]


def normed_kernel(place, r0, r1, r2, r3, reply, gates, w_out, normed, out, states):
    mine = place[0]
    for slot, r in enumerate((r0, r1, r2, r3)):
        states[mine ^ slot] = r[...]
    for h in range(VH):
        core = dot3(reply[h, :, :DK], states[h]) + reply[h, :, DK:]
        scale = lax.rsqrt(jnp.mean(core * core, -1, keepdims=True) + EPS)
        normed[:, h * DV : (h + 1) * DV] = (core * scale * gates[:, h * DV : (h + 1) * DV]).astype(BF16)
    for step in range(4):
        out[step] = block_product(normed, w_out, place, step, 1 - place[3])


def block_product(normed, w_out, place, step, core):
    start = pl.multiple_of((((place[2] + step) & 3) * 2 + core) * 256, 256)
    return mm(normed[...], w_out[:, pl.ds(start, 256)])


def own_kernel(place, normed, w_out, own):
    for step in range(4):
        own[step] = block_product(normed, w_out, place, step, place[3])


def arr(*shape, dtype=F32):
    return jax.ShapeDtypeStruct(shape, dtype)


def swap(v, axis, size, mask):
    return lax.ppermute(v, axis, [(i, i ^ mask) for i in range(size)])


def shift(v, axis, size, step):
    return lax.ppermute(v, axis, [(i, (i + step) % size) for i in range(size)])


def forward(v, axis, size, step):
    return lax.ppermute(v, axis, [(i, i + step) for i in range(size - step)])


def local(tokens, w_qk, w_vz, w_ab, conv_qk, conv_v, a_log, dt_bias, beta_bias, norm_gain, w_out):
    y, z = lax.axis_index("y"), lax.axis_index("z")
    x, core = lax.axis_index("x"), lax.axis_index("core")
    place = jnp.stack([z & 3, z >> 2, x, core]).astype(jnp.int32)

    tail = tokens[SEG - 4 :].astype(F32)
    halo = lax.ppermute(tail, ("y", "z"), [(i, i + 1) for i in range(31)])
    flat_qk = w_qk.reshape(w_qk.shape[0], 2 * QKH * DK)
    flat_vz = w_vz.reshape(w_vz.shape[0], 2 * VH * DV)
    ab = w_ab.transpose(1, 2, 0)
    width = tokens.shape[1]
    half_of = lambda size, c: pl.BlockSpec((width, size), lambda i: (0, c))

    def segment(own_group):
        return pl.pallas_call(
            functools.partial(segment_kernel, own_group),
            grid=(1,),
            out_shape=[arr(DK, 256)] * 2 + [arr(SEG, DK), arr(2, SEG, 256), arr(SEG, 8)],
            in_specs=[SMEM] * 4 + [VMEM, VMEM, VMEM, half_of(VH * DV, 0)] + [VMEM] * 3,
            out_specs=[VMEM] * 5,
            scratch_shapes=[
                pltpu.VMEM((3, SEG + 8, DK), F32),
                pltpu.VMEM((8, SEG), F32),
                pltpu.VMEM((2, SEG, DV), F32),
            ],
            compiler_params=params(28),
            cost_estimate=pl.CostEstimate(
                flops=6 * 10**9, bytes_accessed=6 * 10**6, transcendentals=0
            ),
            name="segment_own" if own_group else "segment_other",
        )(place, a_log, dt_bias, beta_bias, tokens, halo, flat_qk, flat_vz, conv_qk, conv_v, ab)

    far = segment(False)
    near = segment(True)
    got = [near[0], swap(near[1], "z", 8, 1), swap(far[0], "z", 8, 2), swap(far[1], "z", 8, 3)]
    reply, gates = pl.pallas_call(
        reply_kernel,
        grid=(1,),
        out_shape=[arr(VH, SEG, 256), arr(SEG, VH * DV)],
        in_specs=[SMEM, VMEM, VMEM, half_of(QKH * DK, 0), half_of(VH * DV, 1)] + [VMEM] * 8,
        out_specs=[VMEM] * 2,
        scratch_shapes=[pltpu.VMEM((2, SEG + 8, DK), F32), pltpu.VMEM((QKH, SEG, DK), F32)],
        compiler_params=params(28),
        cost_estimate=pl.CostEstimate(flops=4 * 10**9, bytes_accessed=3 * 10**6, transcendentals=0),
        name="reply",
    )(place, tokens, halo, flat_qk, flat_vz, conv_qk, norm_gain.reshape(1, DV), *near[2:], *far[2:])

    far_pair = pl.pallas_call(
        pair_kernel,
        out_shape=arr(DK, 256),
        in_specs=[SMEM] + [VMEM] * 2,
        out_specs=VMEM,
        compiler_params=params(16),
        name="pair",
    )(place, *got[2:])
    total, first_pair = pl.pallas_call(
        quad_kernel,
        out_shape=[arr(DK, 256)] * 2,
        in_specs=[SMEM] + [VMEM] * 3,
        out_specs=[VMEM] * 2,
        compiler_params=params(16),
        name="quad",
    )(place, got[0], got[1], far_pair)
    prefixes = pl.pallas_call(
        prefix_kernel,
        out_shape=arr(3, DK, 256),
        in_specs=[SMEM] + [VMEM] * 5,
        out_specs=VMEM,
        compiler_params=params(16),
        name="prefix",
    )(place, *got, first_pair)
    other = swap(total, "z", 8, 4)
    row = pl.pallas_call(
        row_kernel,
        out_shape=arr(DK, 256),
        in_specs=[SMEM] + [VMEM] * 4,
        out_specs=VMEM,
        compiler_params=params(16),
        name="row",
    )(place, total, other, gates, prefixes)
    rows = [forward(row, "y", 4, d) for d in (1, 2, 3)]
    early = pl.pallas_call(
        early_kernel,
        out_shape=arr(DK, DV),
        in_specs=[VMEM] * 2,
        out_specs=VMEM,
        compiler_params=params(16),
        name="early",
    )(*rows[1:])
    states = pl.pallas_call(
        state_kernel,
        out_shape=[arr(DK, DV)] * 4,
        in_specs=[SMEM] + [VMEM] * 4,
        out_specs=[VMEM] * 4,
        scratch_shapes=[pltpu.VMEM((4, DK, DV), F32)],
        compiler_params=params(16),
        name="state",
    )(place, rows[0], early, other, prefixes)
    came = [states[0]] + [swap(states[m], "z", 8, m) for m in (1, 2, 3)]

    normed, for_twin = pl.pallas_call(
        normed_kernel,
        out_shape=[arr(SEG, VH * DV, dtype=BF16), arr(4, SEG, 256)],
        in_specs=[SMEM] + [VMEM] * 7,
        out_specs=[VMEM] * 2,
        scratch_shapes=[pltpu.VMEM((4, DK, DV), F32)],
        compiler_params=params(24),
        name="normed",
    )(place, *came, reply, gates, w_out)
    from_twin = swap(for_twin, "core", 2, 1)
    own = pl.pallas_call(
        own_kernel,
        out_shape=arr(4, SEG, 256),
        in_specs=[SMEM] + [VMEM] * 2,
        out_specs=VMEM,
        compiler_params=params(24),
        cost_estimate=pl.CostEstimate(flops=10**9, bytes_accessed=3 * 10**6, transcendentals=0),
        name="own",
    )(place, normed, w_out)

    from_left = shift(own[2, :HALF] + from_twin[2, :HALF], "x", 4, 1)
    from_right = shift(own[2, HALF:] + from_twin[2, HALF:], "x", 4, -1)
    right = own[1] + from_twin[1]
    left = own[3] + from_twin[3]
    to_right = jnp.concatenate([right[:HALF] + from_left, right[HALF:]], 0)
    to_left = jnp.concatenate([left[:HALF], left[HALF:] + from_right], 0)
    last_left = shift(to_right, "x", 4, 1)
    last_right = shift(to_left, "x", 4, -1)
    return ((own[0] + from_twin[0]) + (last_right + last_left)).astype(BF16)


def solution(mesh):
    split = Mesh(mesh.devices.reshape(4, 8, 4, 2), ("y", "z", "x", "core"))
    seq, head = ("y", "z"), ("x", "core")
    in_specs = (
        P(seq, None),
        P(None, None, head),
        P(None, None, head),
        P(None, None, head),
        P(None, None, head),
        P(None, head),
        P(head),
        P(head),
        P(head),
        P(),
        P(head, None),
    )
    return jax.shard_map(
        local, mesh=split, in_specs=in_specs, out_specs=P(seq, head), check_vma=False
    )
```

```python
import functools

import jax
import jax.numpy as jnp
from jax import lax
from jax.experimental import pallas as pl
from jax.experimental.pallas import tpu as pltpu
from jax.sharding import Mesh, PartitionSpec as P

F32 = jnp.float32
BF16 = jnp.bfloat16
DK = 128
DV = 128
HALF = 128
SEG = 256
VH = 4
QKH = 2
EPS = 1e-06
FLOOR = -110.0

VMEM = pl.BlockSpec(memory_space=pltpu.VMEM)
SMEM = pl.BlockSpec(memory_space=pltpu.SMEM)


def params(mib):
    return pltpu.CompilerParams(vmem_limit_bytes=mib * 1024 * 1024)


def split2(x):
    hi = x.astype(BF16)
    return hi, (x - hi.astype(F32)).astype(BF16)


def split3(x):
    hi = x.astype(BF16)
    rest = x - hi.astype(F32)
    mid = rest.astype(BF16)
    return hi, mid, (rest - mid.astype(F32)).astype(BF16)


def mm(a, b):
    return jnp.dot(a, b, preferred_element_type=F32)


def mm_nt(a, b):
    return lax.dot_general(a, b, (((1,), (1,)), ((), ())), preferred_element_type=F32)


def dot3(a, b):
    ah, al = split2(a)
    bh, bl = split2(b)
    return mm(jnp.concatenate([ah, al, ah], 1), jnp.concatenate([bh, bh, bl], 0))


def dot3_nt(a, b):
    ah, al = split2(a)
    bh, bl = split2(b)
    return mm_nt(jnp.concatenate([ah, al, ah], 1), jnp.concatenate([bh, bh, bl], 1))


def spread_blocks(x):
    zero = jnp.zeros((HALF, HALF), x.dtype)
    return jnp.concatenate(
        [
            jnp.concatenate([x[:, :HALF], zero], 1),
            jnp.concatenate([zero, x[:, HALF:]], 1),
        ],
        0,
    )


def dot3_blocks(a, b):
    ah, al = split2(a)
    bh, bl = split2(b)
    bh, bl = spread_blocks(bh), spread_blocks(bl)
    return mm(jnp.concatenate([ah, al, ah], 1), jnp.concatenate([bh, bh, bl], 0))


def iota2(shape, dim):
    return lax.broadcasted_iota(jnp.int32, shape, dim)


def silu(x):
    return x / (1.0 + jnp.exp(-x))


def softplus(x):
    return jnp.maximum(x, 0.0) + jnp.log1p(jnp.exp(-jnp.abs(x)))


def unit(x):
    return x * lax.rsqrt(jnp.sum(x * x, -1, keepdims=True) + EPS)


def fades(decay_col, lower):
    rows, cols = iota2((SEG, SEG), 0), iota2((SEG, SEG), 1)
    terms = jnp.where(rows > cols, jnp.broadcast_to(decay_col, (SEG, SEG)), 0.0)
    hi, mid, lo = split3(terms)
    return jnp.exp(mm(lower, hi) + mm(lower, mid) + mm(lower, lo))


def lower_ones():
    rows, cols = iota2((SEG, SEG), 0), iota2((SEG, SEG), 1)
    return jnp.where(rows >= cols, 1.0, 0.0).astype(BF16)


def dot3_parts(ah, al, bh, bl):
    return mm(jnp.concatenate([ah, al, ah], 1), jnp.concatenate([bh, bh, bl], 0))


def halo_rows(halo):
    return jnp.concatenate([jnp.zeros((4, halo.shape[1]), F32), halo[...]], 0).astype(BF16)


def conv(pad, block, tap):
    total = None
    for j in range(4):
        term = pad[block, 5 + j : 5 + j + SEG, :] * tap(j)
        total = term if total is None else total + term
    return silu(total)


def project(pad, tok, before, w, block, count):
    full, front = mm(tok, w), mm(before, w)
    for i in range(count):
        pad[block + i, 0:8, :] = front[:, i * 128 : (i + 1) * 128]
        pad[block + i, 8:, :] = full[:, i * 128 : (i + 1) * 128]


def sums_of(parts, weights):
    return jnp.exp(sum(mm(weights, part) for part in parts))


def affine_maps(keys, grams, values, col8, slots):
    rows, cols = iota2((SEG, SEG), 0), iota2((SEG, SEG), 1)
    lower = lower_ones()
    later = jnp.where(rows < cols, 1.0, 0.0).astype(BF16)
    parts = split3(col8)
    growth8, closing8 = sums_of(parts, lower), sums_of(parts, later)
    n = range(len(slots))
    beta = [col8[:, c : c + 1] for c in slots]
    growth = [growth8[:, 4 + c : 5 + c] for c in slots]
    closing = [closing8[:, 4 + c : 5 + c] for c in slots]
    prow, pcol = iota2((HALF, HALF), 0), iota2((HALF, HALF), 1)
    strict = prow > pcol
    eye = jnp.where(prow == pcol, 1.0, 0.0)
    m, corner = [], []
    for i in n:
        u = fades(col8[:, 4 + slots[i] : 5 + slots[i]], lower) * grams[i] * beta[i]
        m += [
            jnp.where(strict, u[:HALF, :HALF], 0.0),
            jnp.where(strict, u[HALF:, HALF:], 0.0),
        ]
        corner.append(u[HALF:, :HALF])
    def within(low, high):
        return ((prow >> high) == (pcol >> high)) & ((prow >> low) != (pcol >> low))

    def mul(a, b):
        return [dot3_parts(*p, *q) for p, q in zip(a, b)]

    def halves(a):
        return [split2(u) for u in a]

    def finish(inv, power):
        square = halves(mul(power, power))
        inv = [u + w for u, w in zip(inv, mul(square, halves(inv)))]
        fourth = halves(mul(square, square))
        return [u + w for u, w in zip(inv, mul(fourth, halves(inv)))]

    near_diag = [jnp.where(within(0, 3), u, 0.0) for u in m]
    t = finish([eye - u for u in near_diag], halves(near_diag))
    ts = halves(t)
    power = halves(mul(ts, halves([jnp.where(within(3, 6), u, 0.0) for u in m])))
    t = finish([u - w for u, w in zip(t, mul(power, ts))], power)
    ts = halves(t)
    inner = halves(mul(halves([jnp.where(within(6, 7), u, 0.0) for u in m]), ts))
    t = [u - w for u, w in zip(t, mul(ts, inner))]
    right = [jnp.concatenate([keys[i] * growth[i], values[i]], 1) * beta[i] for i in n]
    x1 = [dot3(t[2 * i], right[i][:HALF]) for i in n]
    later_half = [dot3(t[2 * i + 1], right[i][HALF:]) for i in n]
    carry = [dot3(t[2 * i + 1], corner[i]) for i in n]
    x2 = [later_half[i] - dot3(carry[i], x1[i]) for i in n]
    ef = [jnp.concatenate([x1[i], x2[i]], 0) for i in n]
    both = [dot3((keys[i] * closing[i]).T, ef[i]) for i in n]
    maps = [
        jnp.concatenate([growth[i][SEG - 1 : SEG] * eye - both[i][:, :DK], both[i][:, DK:]], 1)
        for i in n
    ]
    return maps, ef


def segment_kernel(
    own_group, place, a_log, dt_bias, beta_bias, tokens, halo, w_qk, w_v, taps_qk, taps_v, w_ab,
    out0, out1, k_out, ef_out, cols_out, pad, logits, values,
):
    mine = place[0]
    group = (mine >> 1) if own_group else 1 - (mine >> 1)
    tok = tokens[...]
    before = halo_rows(halo)
    wide = pl.ds(pl.multiple_of(group * 256, 256), 256)
    key_lanes = pl.ds(pl.multiple_of(256 + group * DK, DK), DK)

    def pick(taps, width):
        return jnp.where(group == 1, taps[:, width : 2 * width], taps[:, :width])

    logits[...] = mm_nt(tok, jnp.concatenate([w_ab[0], w_ab[1]], 0)).T
    project(pad, tok, before, w_qk[:, key_lanes], 0, 1)
    project(pad, tok, before, w_v[:, wide], 1, 2)
    betas, decays = [], []
    for slot in range(2):
        h = group * 2 + ((mine & 1) ^ slot)
        betas.append(jax.nn.sigmoid(logits[pl.ds(h, 1), :] + beta_bias[h]))
        rate = jnp.exp(jnp.full((1, SEG), a_log[h], F32))
        decay = -rate * softplus(logits[pl.ds(h + 4, 1), :] + dt_bias[h])
        decays.append(jnp.maximum(decay, FLOOR))
    blank = jnp.zeros((2, SEG), F32)
    col8 = jnp.concatenate(betas + [blank] + decays + [blank], 0).T
    cols_out[...] = col8
    k = unit(conv(pad, 0, lambda j: pick(taps_qk[j, 1:2, :], DK)))
    k_out[...] = k
    gram = dot3_nt(k, k)
    for i in range(2):
        values[i] = conv(
            pad, 1 + i, lambda j: pick(taps_v[j : j + 1, :], 256)[:, i * DV : (i + 1) * DV]
        )
    maps, ef = affine_maps(
        [k, k], [gram, gram], [values[(mine & 1) ^ i] for i in range(2)], col8, (0, 1)
    )
    for i, out in enumerate((out0, out1)):
        out[...] = maps[i]
        ef_out[i] = ef[i]


def reply_kernel(
    place, tokens, halo, w_q, w_z, taps_qk, gain, k_near, ef_near, cols_near, k_far, ef_far, cols_far,
    out, gates, pad, queries,
):
    rows, cols = iota2((SEG, SEG), 0), iota2((SEG, SEG), 1)
    lower = lower_ones()
    mine = place[0]
    tok = tokens[...]
    project(pad, tok, halo_rows(halo), w_q[...], 0, 2)
    z = mm(tok, w_z[...])
    for h in range(VH):
        part = z[:, h * DV : (h + 1) * DV]
        gates[:, h * DV : (h + 1) * DV] = gain[...] * silu(part)
    for g in range(QKH):
        taps = lambda j: taps_qk[j, 0:1, g * DK : (g + 1) * DK]
        queries[g] = unit(conv(pad, g, taps)) * DK ** -0.5
    for side, k, ef, cols8 in ((0, k_near, ef_near, cols_near), (1, k_far, ef_far, cols_far)):
        q = queries[(mine >> 1) ^ side]
        col8 = cols8[...]
        growth8 = sums_of(split3(col8), lower)
        qk = dot3_nt(q, k[...])
        for i in range(2):
            fade = fades(col8[:, 4 + i : 5 + i], lower)
            mixing = jnp.where(rows >= cols, fade * qk, 0.0)
            both = dot3(mixing, ef[i])
            out[mine ^ (2 * side + i)] = jnp.concatenate(
                [q * growth8[:, 4 + i : 5 + i] - both[:, :DK], both[:, DK:]], 1
            )


def after(second, first):
    prod = dot3(second[:, :DK], first)
    return jnp.concatenate([prod[:, :DK], prod[:, DK:] + second[:, DK:]], 1)


def spot_of(place):
    return place[0] ^ (3 * place[1])


def pair_kernel(place, r2, r3, out):
    odd = (spot_of(place) & 1) == 1
    out[...] = after(
        jnp.where(odd, r2[...], r3[...]), jnp.where(odd, r3[...], r2[...])
    )


def quad_kernel(place, r0, r1, far, total, first_pair):
    spot = spot_of(place)
    odd, upper = (spot & 1) == 1, spot >= 2
    near = after(jnp.where(odd, r0[...], r1[...]), jnp.where(odd, r1[...], r0[...]))
    first, second = jnp.where(upper, far[...], near), jnp.where(upper, near, far[...])
    total[...] = after(second, first)
    first_pair[...] = first


def prefix_kernel(place, r0, r1, r2, r3, first_pair, prefixes):
    spot = spot_of(place)
    odd, upper = (spot & 1) == 1, spot >= 2
    near_first = jnp.where(odd, r1[...], r0[...])
    far_first = jnp.where(odd, r3[...], r2[...])
    prefixes[0] = jnp.where(upper, far_first, near_first)
    prefixes[1] = first_pair[...]
    prefixes[2] = after(jnp.where(upper, near_first, far_first), first_pair[...])


def row_kernel(place, own, other, after_reply, after_prefixes, out):
    behind = place[1] == 1
    first = jnp.where(behind, other[...], own[...])
    second = jnp.where(behind, own[...], other[...])
    out[...] = after(second, first)


def early_kernel(y2, y3, out):
    out[...] = dot3(y2[:, :DK], y3[:, DK:]) + y2[:, DK:]


def state_kernel(place, y1, early, other, prefixes, out0, out1, out2, out3, states):
    s = dot3(y1[:, :DK], early[...]) + y1[:, DK:]
    s = jnp.where(place[1] == 1, dot3(other[:, :DK], s) + other[:, DK:], s)
    states[0] = s
    for j in range(3):
        states[j + 1] = dot3(prefixes[j, :, :DK], s) + prefixes[j, :, DK:]
    spot = spot_of(place)
    for slot, out in enumerate((out0, out1, out2, out3)):
        out[...] = states[spot ^ slot]


def normed_kernel(place, r0, r1, r2, r3, reply, gates, w_out, normed, out, states):
    mine = place[0]
    for slot, r in enumerate((r0, r1, r2, r3)):
        states[mine ^ slot] = r[...]
    for h in range(VH):
        core = dot3(reply[h, :, :DK], states[h]) + reply[h, :, DK:]
        scale = lax.rsqrt(jnp.mean(core * core, -1, keepdims=True) + EPS)
        normed[:, h * DV : (h + 1) * DV] = (core * scale * gates[:, h * DV : (h + 1) * DV]).astype(BF16)
    for step in range(4):
        out[step] = block_product(normed, w_out, place, step, 1 - place[3])


def block_product(normed, w_out, place, step, core):
    start = pl.multiple_of((((place[2] + step) & 3) * 2 + core) * 256, 256)
    return mm(normed[...], w_out[:, pl.ds(start, 256)])


def own_kernel(place, normed, w_out, own):
    for step in range(4):
        own[step] = block_product(normed, w_out, place, step, place[3])


def arr(*shape, dtype=F32):
    return jax.ShapeDtypeStruct(shape, dtype)


def swap(v, axis, size, mask):
    return lax.ppermute(v, axis, [(i, i ^ mask) for i in range(size)])


def shift(v, axis, size, step):
    return lax.ppermute(v, axis, [(i, (i + step) % size) for i in range(size)])


def forward(v, axis, size, step):
    return lax.ppermute(v, axis, [(i, i + step) for i in range(size - step)])


def local(tokens, w_qk, w_vz, w_ab, conv_qk, conv_v, a_log, dt_bias, beta_bias, norm_gain, w_out):
    y, z = lax.axis_index("y"), lax.axis_index("z")
    x, core = lax.axis_index("x"), lax.axis_index("core")
    place = jnp.stack([(z & 3) ^ (3 * (z >> 2)), z >> 2, x, core]).astype(jnp.int32)

    tail = tokens[SEG - 4 :].astype(F32)
    halo = lax.ppermute(tail, ("y", "z"), [(i, i + 1) for i in range(31)])
    flat_qk = w_qk.reshape(w_qk.shape[0], 2 * QKH * DK)
    flat_vz = w_vz.reshape(w_vz.shape[0], 2 * VH * DV)
    ab = w_ab.transpose(1, 2, 0)
    width = tokens.shape[1]
    half_of = lambda size, c: pl.BlockSpec((width, size), lambda i: (0, c))

    def segment(own_group):
        return pl.pallas_call(
            functools.partial(segment_kernel, own_group),
            grid=(1,),
            out_shape=[arr(DK, 256)] * 2 + [arr(SEG, DK), arr(2, SEG, 256), arr(SEG, 8)],
            in_specs=[SMEM] * 4 + [VMEM, VMEM, VMEM, half_of(VH * DV, 0)] + [VMEM] * 3,
            out_specs=[VMEM] * 5,
            scratch_shapes=[
                pltpu.VMEM((3, SEG + 8, DK), F32),
                pltpu.VMEM((8, SEG), F32),
                pltpu.VMEM((2, SEG, DV), F32),
            ],
            compiler_params=params(28),
            cost_estimate=pl.CostEstimate(
                flops=6 * 10**9, bytes_accessed=6 * 10**6, transcendentals=0
            ),
            name="segment_own" if own_group else "segment_other",
        )(place, a_log, dt_bias, beta_bias, tokens, halo, flat_qk, flat_vz, conv_qk, conv_v, ab)

    far = segment(False)
    near = segment(True)
    got = [near[0], swap(near[1], "z", 8, 1), swap(far[0], "z", 8, 2), swap(far[1], "z", 8, 3)]
    reply, gates = pl.pallas_call(
        reply_kernel,
        grid=(1,),
        out_shape=[arr(VH, SEG, 256), arr(SEG, VH * DV)],
        in_specs=[SMEM, VMEM, VMEM, half_of(QKH * DK, 0), half_of(VH * DV, 1)] + [VMEM] * 8,
        out_specs=[VMEM] * 2,
        scratch_shapes=[pltpu.VMEM((2, SEG + 8, DK), F32), pltpu.VMEM((QKH, SEG, DK), F32)],
        compiler_params=params(28),
        cost_estimate=pl.CostEstimate(flops=4 * 10**9, bytes_accessed=3 * 10**6, transcendentals=0),
        name="reply",
    )(place, tokens, halo, flat_qk, flat_vz, conv_qk, norm_gain.reshape(1, DV), *near[2:], *far[2:])

    far_pair = pl.pallas_call(
        pair_kernel,
        out_shape=arr(DK, 256),
        in_specs=[SMEM] + [VMEM] * 2,
        out_specs=VMEM,
        compiler_params=params(16),
        name="pair",
    )(place, *got[2:])
    total, first_pair = pl.pallas_call(
        quad_kernel,
        out_shape=[arr(DK, 256)] * 2,
        in_specs=[SMEM] + [VMEM] * 3,
        out_specs=[VMEM] * 2,
        compiler_params=params(16),
        name="quad",
    )(place, got[0], got[1], far_pair)
    prefixes = pl.pallas_call(
        prefix_kernel,
        out_shape=arr(3, DK, 256),
        in_specs=[SMEM] + [VMEM] * 5,
        out_specs=VMEM,
        compiler_params=params(16),
        name="prefix",
    )(place, *got, first_pair)
    other = swap(total, "z", 8, 7)
    row = pl.pallas_call(
        row_kernel,
        out_shape=arr(DK, 256),
        in_specs=[SMEM] + [VMEM] * 4,
        out_specs=VMEM,
        compiler_params=params(16),
        name="row",
    )(place, total, other, gates, prefixes)
    rows = [forward(row, "y", 4, d) for d in (1, 2, 3)]
    early = pl.pallas_call(
        early_kernel,
        out_shape=arr(DK, DV),
        in_specs=[VMEM] * 2,
        out_specs=VMEM,
        compiler_params=params(16),
        name="early",
    )(*rows[1:])
    states = pl.pallas_call(
        state_kernel,
        out_shape=[arr(DK, DV)] * 4,
        in_specs=[SMEM] + [VMEM] * 4,
        out_specs=[VMEM] * 4,
        scratch_shapes=[pltpu.VMEM((4, DK, DV), F32)],
        compiler_params=params(16),
        name="state",
    )(place, rows[0], early, other, prefixes)
    came = [states[0]] + [swap(states[m], "z", 8, m) for m in (1, 2, 3)]

    normed, for_twin = pl.pallas_call(
        normed_kernel,
        out_shape=[arr(SEG, VH * DV, dtype=BF16), arr(4, SEG, 256)],
        in_specs=[SMEM] + [VMEM] * 7,
        out_specs=[VMEM] * 2,
        scratch_shapes=[pltpu.VMEM((4, DK, DV), F32)],
        compiler_params=params(24),
        name="normed",
    )(place, *came, reply, gates, w_out)
    from_twin = swap(for_twin, "core", 2, 1)
    own = pl.pallas_call(
        own_kernel,
        out_shape=arr(4, SEG, 256),
        in_specs=[SMEM] + [VMEM] * 2,
        out_specs=VMEM,
        compiler_params=params(24),
        cost_estimate=pl.CostEstimate(flops=10**9, bytes_accessed=3 * 10**6, transcendentals=0),
        name="own",
    )(place, normed, w_out)

    from_left = shift(own[2, :HALF] + from_twin[2, :HALF], "x", 4, 1)
    from_right = shift(own[2, HALF:] + from_twin[2, HALF:], "x", 4, -1)
    right = own[1] + from_twin[1]
    left = own[3] + from_twin[3]
    to_right = jnp.concatenate([right[:HALF] + from_left, right[HALF:]], 0)
    to_left = jnp.concatenate([left[:HALF], left[HALF:] + from_right], 0)
    last_left = shift(to_right, "x", 4, 1)
    last_right = shift(to_left, "x", 4, -1)
    return ((own[0] + from_twin[0]) + (last_right + last_left)).astype(BF16)


def solution(mesh):
    split = Mesh(mesh.devices.reshape(4, 8, 4, 2), ("y", "z", "x", "core"))
    seq, head = ("y", "z"), ("x", "core")
    in_specs = (
        P(seq, None),
        P(None, None, head),
        P(None, None, head),
        P(None, None, head),
        P(None, None, head),
        P(None, head),
        P(head),
        P(head),
        P(head),
        P(),
        P(head, None),
    )
    return jax.shard_map(
        local, mesh=split, in_specs=in_specs, out_specs=P(seq, head), check_vma=False
    )
```
